32 devices in a mesh: panel: 8 (over z, core), case: 4 (over y, x).
Axes of the slice: x: 2, y: 2, z: 4, core: 2. Of those that a mesh axis runs over, the one named last changes fastest.
Arguments:
- strengths: bfloat16 [32, 49152], P('panel', 'case'), may hold values from -6 to 6
- blocks: bfloat16 [1024, 256, 256], P(('panel', 'case')), may hold values from -0.21875 to 0.21875
- pattern: int32 [1024, 3], P(('panel', 'case')), may hold values from -1 to 191, as said below
- level_gain: float32 [8], replicated, may hold values from 0.25 to 2
Outputs:
- forward_one: bfloat16 [32, 49152], P('case', 'panel')
- adjoint_one: bfloat16 [32, 49152], P('panel', 'case')
- forward_two: bfloat16 [32, 49152], P('case', 'panel')
- adjoint_two: bfloat16 [32, 49152], P('panel', 'case')
The draws below stay inside these ranges and needn't reach their ends.
Inputs may be any that keep to these rules, and one draw needn't show every extreme that they name: `pattern`: entries come in runs of 32, one run for each pair of a panel index p and a case index c, ordered with p slowest; a run's row blocks lie in p * 24 to (p + 1) * 24 - 1 and its column blocks in c * 48 to (c + 1) * 48 - 1; no (row block, column block) pair appears twice; levels lie in 0 to 7; an empty slot is (-1, -1, -1), a run holds its stored blocks first and its empty slots after them, every run holds at least one stored block and some run is full.
All inputs are finite; a program needn't handle non-finite values.
Results may differ from the reference program's by a relative error of at most 0.024.
Values may be sent and summed in bfloat16 or wider, within the bound.
No kernel may reach another device: no remote copies, remote signals or barrier semaphores. Data moves between devices by JAX's collectives and lax.ppermute only.
A program may use at most 64 MiB of HBM per device.

```python
import math
import jax
import jax.numpy as jnp
from jax import lax

B = 256
CASES = 32
LEVELS = 8
ROWB_DEV = 24
BLK_DEV = 32
COLB_DEV = 48
NBLK = 1024
NPAN = 49152
N_PANEL = 8
N_CASE = 4


def draw_pattern(key, part):
    device_count = N_PANEL * N_CASE
    tile_size = ROWB_DEV * COLB_DEV
    key_order, key_count, key_full, key_level = jax.random.split(jax.random.fold_in(key, 17), 4)
    scores = jax.random.randint(key_order, (device_count, tile_size), 0, 1 << 20)
    scores = scores * tile_size + jnp.arange(tile_size, dtype=jnp.int32)[None, :]
    scores = scores.at[:, tile_size - 1].set(-1)
    order = jnp.argsort(scores, axis=1, stable=True)[:, :BLK_DEV].astype(jnp.int32)
    row_local = order // COLB_DEV
    col_local = order % COLB_DEV
    counts = jax.random.randint(key_count, (device_count,), max(1, BLK_DEV // 4), BLK_DEV + 1)
    full_device = jax.random.randint(key_full, (), 0, device_count)
    counts = jnp.where(jnp.arange(device_count) == full_device, BLK_DEV, counts)
    is_live = jnp.arange(BLK_DEV)[None, :] < counts[:, None]
    device_ids = jnp.arange(device_count, dtype=jnp.int32)
    panel_ids = device_ids // N_CASE
    case_ids = device_ids % N_CASE
    row_block = panel_ids[:, None] * ROWB_DEV + row_local
    col_block = case_ids[:, None] * COLB_DEV + col_local
    level_ids = jax.random.randint(key_level, (device_count, BLK_DEV), 0, LEVELS)
    stacked = jnp.stack([row_block, col_block, level_ids], axis=2)
    stacked = jnp.where(is_live[:, :, None], stacked, -1)
    return stacked.reshape(device_count * BLK_DEV, 3).astype(jnp.int32)


def level_of(own_key, shape, shards, smallest, top_value):
    level, own = 1.0, jax.random.fold_in(own_key, 6)
    for position, parts in shards:
        draws = jnp.exp(jax.random.uniform(jax.random.fold_in(own, position), (parts,), jnp.float32, smallest / len(shards), top_value / len(shards)))
        level = level * jnp.repeat(draws, shape[position] // parts).reshape([-1 if axis == position else 1 for axis in range(len(shape))])
    return level


def centred(key, dims, width, most, cuts=(), held_as=jnp.bfloat16):
    drawn = width * jax.random.normal(key, dims, jnp.float32)
    if cuts:
        drawn = drawn * level_of(key, dims, cuts, -0.22, 0.18)
    return jnp.clip(drawn, -most, most).astype(held_as)


def setup_inputs(seed: int = 0) -> dict:
    arg_keys = jax.random.split(jax.random.key(seed), 5)
    return {
        "strengths": centred(arg_keys[0], (CASES, NPAN), 1.0, 6.0, ((0, 8), (1, 4))),
        "blocks": centred(arg_keys[1], (NBLK, B, B), (B * N_CASE * BLK_DEV * 5 // (8 * ROWB_DEV)) ** -0.5, 0.21875, ((0, 32),)),
        "pattern": draw_pattern(jax.random.fold_in(arg_keys[4], 71), 0),
        "level_gain": jnp.clip(jnp.exp(jax.random.uniform(arg_keys[3], (LEVELS,), jnp.float32, math.log(0.25), math.log(2.0))), 0.25, 2.0),
    }


def level_scale(pattern, level_gain):
    level_ids = jnp.arange(LEVELS, dtype=jnp.int32)
    chosen = jnp.where(pattern[:, 2:3] == level_ids[None, :], level_gain[None, :], jnp.float32(0.0))
    return jnp.sum(chosen, axis=1)


def group_partial(values, group_blocks, group_pattern, group_scale, adjoint):
    running = jnp.zeros((CASES, NPAN), jnp.float32)

    def advance(carry, record):
        tile_block, entries, factor = record
        row_at = jnp.maximum(entries[0], 0).astype(jnp.int32) * B
        col_at = jnp.maximum(entries[1], 0).astype(jnp.int32) * B
        matrix = tile_block.astype(jnp.float32)
        if adjoint:
            source = lax.dynamic_slice_in_dim(values, row_at, B, 1).astype(jnp.float32)
            product_term = jnp.dot(source, matrix, precision=lax.Precision.HIGHEST) * factor
            target = col_at
        else:
            source = lax.dynamic_slice_in_dim(values, col_at, B, 1).astype(jnp.float32)
            product_term = jnp.dot(source, matrix.T, precision=lax.Precision.HIGHEST) * factor
            target = row_at
        current = lax.dynamic_slice_in_dim(carry, target, B, 1)
        carry = lax.dynamic_update_slice_in_dim(carry, current + product_term, target, 1)
        return carry, None

    running, _ = lax.scan(advance, running, (group_blocks, group_pattern, group_scale))
    return running


def apply_matrix(values, blocks, pattern, block_scale, adjoint):
    blocks_runs = blocks.reshape(N_PANEL, N_CASE, BLK_DEV, B, B)
    pattern_runs = pattern.reshape(N_PANEL, N_CASE, BLK_DEV, 3)
    scale_runs = block_scale.reshape(N_PANEL, N_CASE, BLK_DEV)
    group_axis = 0 if adjoint else 1
    group_count = N_PANEL if adjoint else N_CASE

    def one_group(total, group):
        group_blocks = lax.dynamic_index_in_dim(blocks_runs, group, group_axis, keepdims=False).reshape(-1, B, B)
        group_pattern = lax.dynamic_index_in_dim(pattern_runs, group, group_axis, keepdims=False).reshape(-1, 3)
        group_scale = lax.dynamic_index_in_dim(scale_runs, group, group_axis, keepdims=False).reshape(-1)
        partial_value = group_partial(values, group_blocks, group_pattern, group_scale, adjoint)
        rounded = lax.optimization_barrier(partial_value.astype(jnp.bfloat16)).astype(jnp.float32)
        return total + rounded, None

    total, _ = lax.scan(one_group, jnp.zeros((CASES, NPAN), jnp.float32), jnp.arange(group_count, dtype=jnp.int32))
    return total.astype(jnp.bfloat16)


def reference(strengths, blocks, pattern, level_gain):
    block_scale = level_scale(pattern, level_gain)
    forward_one = apply_matrix(strengths, blocks, pattern, block_scale, False)
    adjoint_one = apply_matrix(forward_one, blocks, pattern, block_scale, True)
    forward_two = apply_matrix(adjoint_one, blocks, pattern, block_scale, False)
    adjoint_two = apply_matrix(forward_two, blocks, pattern, block_scale, True)
    return forward_one, adjoint_one, forward_two, adjoint_two
```

```python
import jax
import jax.numpy as jnp
from jax import lax
from jax.sharding import PartitionSpec as P

B = 256


def swap(value, axis, offset):
    count = lax.axis_size(axis)
    return lax.ppermute(value, axis, [(i, i ^ offset) for i in range(count)])


def pick(pieces, index):
    return lax.dynamic_index_in_dim(pieces, index, 0, keepdims=False)


def place(parts, order, offsets):
    me = order
    stacked = jnp.stack(parts)
    out = jnp.zeros_like(stacked)
    for part, offset in zip(parts, offsets):
        out = lax.dynamic_update_slice_in_dim(out, part[None], me ^ offset, 0)
    return out


def gather_direct(piece, axis):
    count = lax.axis_size(axis)
    me = lax.axis_index(axis)
    parts = [piece] + [swap(piece, axis, k) for k in range(1, count)]
    return place(parts, me, range(count))


def gather_pairs(piece, axis):
    count = lax.axis_size(axis)
    me = lax.axis_index(axis)
    same = [piece] + [swap(piece, axis, k) for k in range(2, count, 2)]
    other = [swap(part, axis, 1) for part in same]
    parts = same + other
    offsets = list(range(0, count, 2)) + [k ^ 1 for k in range(0, count, 2)]
    return place(parts, me, offsets)


def scatter_direct(pieces, axis):
    count = lax.axis_size(axis)
    me = lax.axis_index(axis)
    arrived = [swap(pick(pieces, me ^ k), axis, k) for k in range(1, count)]
    total = pick(pieces, me).astype(jnp.float32)
    for part in arrived:
        total = total + part.astype(jnp.float32)
    return total.astype(pieces.dtype)


def scatter_pairs(pieces, axis):
    count = lax.axis_size(axis)
    me = lax.axis_index(axis)
    side = me & 1
    paired = pieces.reshape(count // 2, 2, *pieces.shape[1:])
    mine = lax.dynamic_index_in_dim(paired, side, 1, keepdims=False)
    theirs = lax.dynamic_index_in_dim(paired, 1 - side, 1, keepdims=False)
    summed = (mine.astype(jnp.float32) + swap(theirs, axis, 1).astype(jnp.float32)).astype(pieces.dtype)
    place_of = me // 2
    arrived = [swap(pick(summed, place_of ^ k), axis, 2 * k) for k in range(1, count // 2)]
    total = pick(summed, place_of).astype(jnp.float32)
    for part in arrived:
        total = total + part.astype(jnp.float32)
    return total.astype(pieces.dtype)


def shards(strengths, blocks, pattern, level_gain):
    n_panel = lax.axis_size("panel")
    n_case = lax.axis_size("case")
    cases = strengths.shape[0] * n_panel
    col_blocks = strengths.shape[1] // B
    row_blocks = col_blocks * n_case // n_panel
    row_local = pattern[:, 0] - lax.axis_index("panel") * row_blocks
    col_local = pattern[:, 1] - lax.axis_index("case") * col_blocks
    level_ids = jnp.arange(level_gain.shape[0], dtype=jnp.int32)
    block_scale = jnp.sum(
        jnp.where(pattern[:, 2:3] == level_ids[None, :], level_gain[None, :], jnp.float32(0.0)),
        axis=1,
    )
    row_pick = row_local[:, None] == jnp.arange(row_blocks, dtype=jnp.int32)[None, :]
    col_pick = col_local[:, None] == jnp.arange(col_blocks, dtype=jnp.int32)[None, :]

    def forward_terms(portion):
        tiled = portion.reshape(cases, col_blocks, B)
        picked = jnp.einsum(
            "sc,kcm->skm", col_pick.astype(jnp.bfloat16), tiled, preferred_element_type=jnp.float32
        ).astype(jnp.bfloat16)
        contrib = (
            jnp.einsum("skm,snm->skn", picked, blocks, preferred_element_type=jnp.float32)
            * block_scale[:, None, None]
        )
        row_terms = jnp.einsum(
            "sr,skn->krn", row_pick.astype(jnp.float32), contrib, precision=lax.Precision.HIGHEST
        )
        return row_terms.reshape(cases, row_blocks * B).astype(jnp.bfloat16)

    def adjoint_terms(portion):
        tiled = portion.reshape(cases, row_blocks, B)
        picked = jnp.einsum(
            "sr,krn->skn", row_pick.astype(jnp.bfloat16), tiled, preferred_element_type=jnp.float32
        ).astype(jnp.bfloat16)
        contrib = (
            jnp.einsum("skn,snm->skm", picked, blocks, preferred_element_type=jnp.float32)
            * block_scale[:, None, None]
        )
        col_terms = jnp.einsum(
            "sc,skm->kcm", col_pick.astype(jnp.float32), contrib, precision=lax.Precision.HIGHEST
        )
        return col_terms.reshape(cases, col_blocks * B).astype(jnp.bfloat16)

    def by_case(terms):
        return terms.reshape(n_case, cases // n_case, -1)

    def by_panel(terms):
        return terms.reshape(n_panel, cases // n_panel, -1)

    def flat(gathered):
        return gathered.reshape(cases, -1)

    first = flat(gather_pairs(strengths, "panel"))
    forward_one = scatter_direct(by_case(forward_terms(first)), "case")
    forward_full = flat(gather_direct(forward_one, "case"))
    adjoint_one = scatter_pairs(by_panel(adjoint_terms(forward_full)), "panel")
    adjoint_full = flat(gather_pairs(adjoint_one, "panel"))
    forward_two = scatter_direct(by_case(forward_terms(adjoint_full)), "case")
    second_full = flat(gather_direct(forward_two, "case"))
    adjoint_two = scatter_pairs(by_panel(adjoint_terms(second_full)), "panel")
    return (forward_one, adjoint_one, forward_two, adjoint_two)


def solution(mesh):
    in_specs = (
        P("panel", "case"),
        P(("panel", "case"), None, None),
        P(("panel", "case"), None),
        P(),
    )
    out_specs = (P("case", "panel"), P("panel", "case"), P("case", "panel"), P("panel", "case"))
    return jax.shard_map(shards, mesh=mesh, in_specs=in_specs, out_specs=out_specs, check_vma=False)
```

```python
import jax
import jax.numpy as jnp
from jax import lax
from jax.sharding import PartitionSpec as P

B = 256


def swap(value, axis, offset):
    count = lax.axis_size(axis)
    return lax.ppermute(value, axis, [(i, i ^ offset) for i in range(count)])


def trade(pieces, axis, groups=None):
    return lax.all_to_all(pieces, axis, 0, 0, tiled=True, axis_index_groups=groups)


def same_core(count):
    return [list(range(core, count, 2)) for core in range(2)]


def spread(piece, count):
    return jnp.broadcast_to(piece[None], (count, *piece.shape))


def add_up(parts):
    return jnp.sum(parts.astype(jnp.float32), axis=0).astype(parts.dtype)


def gather_direct(piece, axis):
    return trade(spread(piece, lax.axis_size(axis)), axis)


def gather_pairs(piece, axis):
    count = lax.axis_size(axis)
    same = trade(spread(piece, count // 2), axis, same_core(count))
    other = swap(same, axis, 1)
    is_odd = (lax.axis_index(axis) & 1) == 1
    pair = jnp.stack([jnp.where(is_odd, other, same), jnp.where(is_odd, same, other)], axis=1)
    return pair.reshape(count, *piece.shape)


def scatter_direct(pieces, axis):
    return add_up(trade(pieces, axis))


def scatter_pairs(pieces, axis):
    count = lax.axis_size(axis)
    side = lax.axis_index(axis) & 1
    paired = pieces.reshape(count // 2, 2, *pieces.shape[1:])
    mine = lax.dynamic_index_in_dim(paired, side, 1, keepdims=False)
    theirs = lax.dynamic_index_in_dim(paired, 1 - side, 1, keepdims=False)
    summed = (mine.astype(jnp.float32) + swap(theirs, axis, 1).astype(jnp.float32)).astype(pieces.dtype)
    return add_up(trade(summed, axis, same_core(count)))


def shards(strengths, blocks, pattern, level_gain):
    n_panel = lax.axis_size("panel")
    n_case = lax.axis_size("case")
    cases = strengths.shape[0] * n_panel
    col_blocks = strengths.shape[1] // B
    row_blocks = col_blocks * n_case // n_panel
    row_local = pattern[:, 0] - lax.axis_index("panel") * row_blocks
    col_local = pattern[:, 1] - lax.axis_index("case") * col_blocks
    level_ids = jnp.arange(level_gain.shape[0], dtype=jnp.int32)
    block_scale = jnp.sum(
        jnp.where(pattern[:, 2:3] == level_ids[None, :], level_gain[None, :], jnp.float32(0.0)),
        axis=1,
    )
    row_pick = row_local[:, None] == jnp.arange(row_blocks, dtype=jnp.int32)[None, :]
    col_pick = col_local[:, None] == jnp.arange(col_blocks, dtype=jnp.int32)[None, :]

    def forward_terms(portion):
        tiled = portion.reshape(cases, col_blocks, B)
        picked = jnp.einsum(
            "sc,kcm->skm", col_pick.astype(jnp.bfloat16), tiled, preferred_element_type=jnp.float32
        ).astype(jnp.bfloat16)
        contrib = (
            jnp.einsum("skm,snm->skn", picked, blocks, preferred_element_type=jnp.float32)
            * block_scale[:, None, None]
        )
        row_terms = jnp.einsum(
            "sr,skn->krn", row_pick.astype(jnp.float32), contrib, precision=lax.Precision.HIGHEST
        )
        return row_terms.reshape(cases, row_blocks * B).astype(jnp.bfloat16)

    def adjoint_terms(portion):
        tiled = portion.reshape(cases, row_blocks, B)
        picked = jnp.einsum(
            "sr,krn->skn", row_pick.astype(jnp.bfloat16), tiled, preferred_element_type=jnp.float32
        ).astype(jnp.bfloat16)
        contrib = (
            jnp.einsum("skn,snm->skm", picked, blocks, preferred_element_type=jnp.float32)
            * block_scale[:, None, None]
        )
        col_terms = jnp.einsum(
            "sc,skm->kcm", col_pick.astype(jnp.float32), contrib, precision=lax.Precision.HIGHEST
        )
        return col_terms.reshape(cases, col_blocks * B).astype(jnp.bfloat16)

    def by_case(terms):
        return terms.reshape(n_case, cases // n_case, -1)

    def by_panel(terms):
        return terms.reshape(n_panel, cases // n_panel, -1)

    def flat(gathered):
        return gathered.reshape(cases, -1)

    first = flat(gather_pairs(strengths, "panel"))
    forward_one = scatter_direct(by_case(forward_terms(first)), "case")
    forward_full = flat(gather_direct(forward_one, "case"))
    adjoint_one = scatter_pairs(by_panel(adjoint_terms(forward_full)), "panel")
    adjoint_full = flat(gather_pairs(adjoint_one, "panel"))
    forward_two = scatter_direct(by_case(forward_terms(adjoint_full)), "case")
    second_full = flat(gather_direct(forward_two, "case"))
    adjoint_two = scatter_pairs(by_panel(adjoint_terms(second_full)), "panel")
    return (forward_one, adjoint_one, forward_two, adjoint_two)


def solution(mesh):
    in_specs = (
        P("panel", "case"),
        P(("panel", "case"), None, None),
        P(("panel", "case"), None),
        P(),
    )
    out_specs = (P("case", "panel"), P("panel", "case"), P("case", "panel"), P("panel", "case"))
    return jax.shard_map(shards, mesh=mesh, in_specs=in_specs, out_specs=out_specs, check_vma=False)
```

```python
import functools

import jax
import jax.numpy as jnp
from jax import lax
from jax.experimental import pallas as pl
from jax.experimental.pallas import tpu as pltpu
from jax.sharding import PartitionSpec as P

B = 256
LANES = 128
PER = B // LANES
COPIES = 4
VMEM_LIMIT = 32 * 1024 * 1024


def swap(value, axis, offset):
    count = lax.axis_size(axis)
    return lax.ppermute(value, axis, [(i, i ^ offset) for i in range(count)])


def add_up(*parts):
    total = parts[0].astype(jnp.float32)
    for part in parts[1:]:
        total = total + part.astype(jnp.float32)
    return total.astype(parts[0].dtype)


def start_blocks(blocks_ref, held, sems):
    share = blocks_ref.shape[0] // COPIES
    copies = []
    for i in range(COPIES):
        span = pl.ds(i * share, share)
        copies.append(pltpu.make_async_copy(blocks_ref.at[span], held.at[span], sems.at[i]))
        copies[-1].start()
    return copies


def slot_of(entry_ref, gain_ref, slot):
    level = entry_ref[slot, 2]
    scale = jnp.where(level >= 0, gain_ref[jnp.maximum(level, 0)], jnp.float32(0.0))
    return entry_ref[slot, 0], entry_ref[slot, 1], scale


def add_products(entry_ref, gain_ref, load, held, copies, total, adjoint):
    total[...] = jnp.zeros_like(total)
    slots = held.shape[0]
    share = slots // COPIES
    for slot in range(slots):
        if slot % share == 0:
            copies[slot // share].wait()
        row, col, scale = slot_of(entry_ref, gain_ref, slot)
        source, target = (row, col) if adjoint else (col, row)
        term = lax.dot_general(
            load(source),
            held[slot],
            (((1,), (0 if adjoint else 1,)), ((), ())),
            preferred_element_type=jnp.float32,
        )
        term = term * scale
        for part in range(PER):
            total[target * PER + part] += term[:, part * LANES : (part + 1) * LANES]


def first_kernel(entry_ref, gain_ref, x_ref, blocks_ref, low_ref, high_ref, held, total, sems):
    copies = start_blocks(blocks_ref, held, sems)

    def load(block):
        return x_ref[:, pl.ds(pl.multiple_of(block * B, B), B)]

    add_products(entry_ref, gain_ref, load, held, copies, total, False)
    half = low_ref.shape[0]
    low_ref[...] = total[:half].astype(low_ref.dtype)
    high_ref[...] = total[half:].astype(high_ref.dtype)


def load_from(x):
    def load(block):
        return jnp.concatenate([x[block * PER + part] for part in range(PER)], axis=1)

    return load


def forward_kernel(ways, entry_ref, gain_ref, place_ref, *refs):
    pieces = refs[: 2 * ways]
    blocks_ref, low_ref, high_ref, held, total, x, sems = refs[2 * ways :]
    copies = start_blocks(blocks_ref, held, sems)
    core, along = place_ref[0], place_ref[1]
    size = pieces[0].shape[0]
    for side in range(2):
        for way in range(ways):
            at = ((core ^ side) * ways + (along ^ way)) * size
            x[pl.ds(at, size)] = pieces[side * ways + way][...]
    add_products(entry_ref, gain_ref, load_from(x), held, copies, total, False)
    half = low_ref.shape[0]
    low_ref[...] = total[:half].astype(low_ref.dtype)
    high_ref[...] = total[half:].astype(high_ref.dtype)


def adjoint_kernel(ways, entry_ref, gain_ref, place_ref, low_ref, high_ref, blocks_ref, mine_ref, theirs_ref, held, total, x, sems):
    copies = start_blocks(blocks_ref, held, sems)
    half = low_ref.shape[0]
    x[:half] = low_ref[...]
    x[half:] = high_ref[...]
    add_products(entry_ref, gain_ref, load_from(x), held, copies, total, True)
    core, along = place_ref[0], place_ref[1]
    size = mine_ref.shape[1]
    for side, out_ref in enumerate((mine_ref, theirs_ref)):
        for way in range(ways):
            at = ((core ^ side) * ways + (along ^ way)) * size
            out_ref[way] = total[pl.ds(at, size)].astype(out_ref.dtype)


def last_kernel(ways, entry_ref, gain_ref, place_ref, low_ref, high_ref, blocks_ref, mine_ref, theirs_ref, held, total, x, sems):
    copies = start_blocks(blocks_ref, held, sems)
    half = low_ref.shape[0]
    x[:half] = low_ref[...]
    x[half:] = high_ref[...]
    add_products(entry_ref, gain_ref, load_from(x), held, copies, total, True)
    core, along = place_ref[0], place_ref[1]
    share = mine_ref.shape[1]
    groups = total.shape[0]
    for own in range(2):

        @pl.when(core == own)
        def _(own=own):
            def write(group, carry):
                lanes = pl.ds(pl.multiple_of(group * LANES, LANES), LANES)
                values = total[group].astype(mine_ref.dtype)
                for index in range(2 * ways):
                    out_ref = mine_ref if index % 2 == own else theirs_ref
                    out_ref[(index // 2) ^ along, :, lanes] = values[index * share : (index + 1) * share]
                return carry

            lax.fori_loop(0, groups, write, 0)


def shards(strengths, blocks, pattern, level_gain):
    n_panel = lax.axis_size("panel")
    n_case = lax.axis_size("case")
    ways = n_panel // 2
    share, width = strengths.shape
    cases = share * n_panel
    slots = blocks.shape[0]
    col_blocks = width // B
    row_blocks = col_blocks * n_case // n_panel
    col_groups = col_blocks * PER
    row_groups = row_blocks * PER
    panel = lax.axis_index("panel")
    case = lax.axis_index("case")
    place = jnp.stack([panel % 2, panel // 2]).astype(jnp.int32)
    first = jnp.stack([panel * row_blocks, case * col_blocks, 0]).astype(jnp.int32)
    entry = jnp.where(pattern[:, 2:3] < 0, jnp.array([0, 0, -1], jnp.int32), pattern - first)
    value = strengths.dtype

    smem = pl.BlockSpec(memory_space=pltpu.SMEM)
    vmem = pl.BlockSpec(memory_space=pltpu.VMEM)
    anywhere = pl.BlockSpec(memory_space=pl.ANY)

    def product(kernel, small, vectors, outs, total_groups, x_groups):
        scratch = [
            pltpu.VMEM(blocks.shape, blocks.dtype),
            pltpu.VMEM((total_groups, cases, LANES), jnp.float32),
        ]
        if x_groups:
            scratch.append(pltpu.VMEM((x_groups, cases, LANES), value))
        scratch.append(pltpu.SemaphoreType.DMA((COPIES,)))
        return pl.pallas_call(
            kernel,
            out_shape=[jax.ShapeDtypeStruct(shape, value) for shape in outs],
            in_specs=[smem] * len(small) + [vmem] * len(vectors) + [anywhere],
            out_specs=[vmem] * len(outs),
            scratch_shapes=scratch,
            compiler_params=pltpu.CompilerParams(vmem_limit_bytes=VMEM_LIMIT),
            cost_estimate=pl.CostEstimate(
                flops=2 * cases * slots * B * B, bytes_accessed=2 * slots * B * B, transcendentals=0
            ),
        )(*small, *vectors, blocks)

    half_rows = [(row_groups // 2, cases, LANES)] * 2
    piece = col_groups // n_panel

    def over_case(low, high):
        bits = [1 << b for b in range(n_case.bit_length() - 1)]
        for one, other in zip(bits, reversed(bits)):
            low_in, high_in = swap(low, "case", one), swap(high, "case", other)
            low, high = add_up(low, low_in), add_up(high, high_in)
        return low, high

    def scatter_panel(mine, theirs):
        summed = add_up(mine, swap(theirs, "panel", 1))
        arrived = [swap(summed[way], "panel", 2 * way) for way in range(1, ways)]
        return add_up(summed[0], *arrived)

    def gather_panel(part):
        same = [part] + [swap(part, "panel", 2 * way) for way in range(1, ways)]
        return same + [swap(one, "panel", 1) for one in same]

    def forward(pieces):
        return product(
            functools.partial(forward_kernel, ways), (entry, level_gain, place), pieces, half_rows, row_groups, col_groups
        )

    def own_cases(low, high):
        whole = jnp.concatenate([low, high])
        own = lax.dynamic_slice_in_dim(whole, case * (cases // n_case), cases // n_case, 1)
        return jnp.swapaxes(own, 0, 1).reshape(cases // n_case, row_groups * LANES)

    def own_share(pieces):
        own = jnp.stack([lax.dynamic_slice_in_dim(one, panel * share, share, 1) for one in pieces])
        own = own.reshape(2, ways, piece, share, LANES)
        own = jnp.where(panel % 2 == 1, own[::-1], own)
        bit = 1
        while bit < ways:
            flipped = own.reshape(2, ways // (2 * bit), 2, bit, piece, share, LANES)[:, :, ::-1].reshape(own.shape)
            own = jnp.where((panel // 2) & bit != 0, flipped, own)
            bit *= 2
        return jnp.moveaxis(own, 3, 0).reshape(share, width)

    same_first = [strengths] + [swap(strengths, "panel", 2 * way) for way in range(1, ways)]
    other_first = [swap(one, "panel", 1) for one in same_first]
    stacked = jnp.zeros((n_panel, share, width), value)
    for side, parts in enumerate((same_first, other_first)):
        for way, one in enumerate(parts):
            stacked = lax.dynamic_update_slice_in_dim(stacked, one[None], panel ^ (2 * way + side), 0)
    low, high = product(first_kernel, (entry, level_gain), [stacked.reshape(cases, width)], half_rows, row_groups, 0)
    low, high = over_case(low, high)
    forward_one = own_cases(low, high)

    mine, theirs = product(
        functools.partial(adjoint_kernel, ways),
        (entry, level_gain, place),
        [low, high],
        [(ways, piece, cases, LANES)] * 2,
        col_groups,
        row_groups,
    )
    pieces = gather_panel(scatter_panel(mine, theirs))
    adjoint_one = own_share(pieces)

    low, high = over_case(*forward(pieces))
    forward_two = own_cases(low, high)

    mine, theirs = product(
        functools.partial(last_kernel, ways),
        (entry, level_gain, place),
        [low, high],
        [(ways, share, width)] * 2,
        col_groups,
        row_groups,
    )
    adjoint_two = scatter_panel(mine, theirs)
    return (forward_one, adjoint_one, forward_two, adjoint_two)


def solution(mesh):
    in_specs = (
        P("panel", "case"),
        P(("panel", "case"), None, None),
        P(("panel", "case"), None),
        P(),
    )
    out_specs = (P("case", "panel"), P("panel", "case"), P("case", "panel"), P("panel", "case"))
    return jax.shard_map(shards, mesh=mesh, in_specs=in_specs, out_specs=out_specs, check_vma=False)
```

```python
import functools

import jax
import jax.numpy as jnp
from jax import lax
from jax.experimental import pallas as pl
from jax.experimental.pallas import tpu as pltpu
from jax.sharding import PartitionSpec as P

B = 256
LANES = 128
PER = B // LANES
VMEM_LIMIT = 24 * 1024 * 1024


def swap(value, axis, offset):
    count = lax.axis_size(axis)
    return lax.ppermute(value, axis, [(i, i ^ offset) for i in range(count)])


def add_up(*parts):
    total = parts[0].astype(jnp.float32)
    for part in parts[1:]:
        total = total + part.astype(jnp.float32)
    return total.astype(parts[0].dtype)


def add_products(entry_ref, gain_ref, load, block_refs, total, adjoint):
    total[...] = jnp.zeros_like(total)
    slots = block_refs[0].shape[0]
    for part, block_ref in enumerate(block_refs):
        for slot in range(slots):
            at = 3 * (part * slots + slot)
            row, col, level = entry_ref[at], entry_ref[at + 1], entry_ref[at + 2]
            scale = jnp.where(level >= 0, gain_ref[jnp.maximum(level, 0)], jnp.float32(0.0))
            source, target = (row, col) if adjoint else (col, row)
            term = lax.dot_general(
                load(source),
                block_ref[slot],
                (((1,), (0 if adjoint else 1,)), ((), ())),
                preferred_element_type=jnp.float32,
            )
            term = term * scale
            for piece in range(PER):
                total[target * PER + piece] += term[:, piece * LANES : (piece + 1) * LANES]


def load_from(x):
    def load(block):
        return jnp.concatenate([x[block * PER + piece] for piece in range(PER)], axis=1)

    return load


def write_halves(total, low_ref, high_ref):
    half = low_ref.shape[0]
    low_ref[...] = total[:half].astype(low_ref.dtype)
    high_ref[...] = total[half:].astype(high_ref.dtype)


def first_kernel(entry_ref, gain_ref, x_ref, own_ref, other_ref, low_ref, high_ref, total):
    def load(block):
        return x_ref[:, pl.ds(pl.multiple_of(block * B, B), B)]

    add_products(entry_ref, gain_ref, load, (own_ref, other_ref), total, False)
    write_halves(total, low_ref, high_ref)


def forward_kernel(ways, entry_ref, gain_ref, place_ref, *refs):
    pieces = refs[:ways]
    own_ref, other_ref, low_ref, high_ref, total, x = refs[ways:]
    along = place_ref[0]
    size = pieces[0].shape[0]
    for way in range(ways):
        x[pl.ds((along ^ way) * size, size)] = pieces[way][...]
    add_products(entry_ref, gain_ref, load_from(x), (own_ref, other_ref), total, False)
    write_halves(total, low_ref, high_ref)


def adjoint_kernel(ways, entry_ref, gain_ref, place_ref, low_ref, high_ref, own_ref, other_ref, *refs):
    total, x = refs[ways:]
    half = low_ref.shape[0]
    x[:half] = low_ref[...]
    x[half:] = high_ref[...]
    add_products(entry_ref, gain_ref, load_from(x), (own_ref, other_ref), total, True)
    along = place_ref[0]
    size = refs[0].shape[0]
    for way in range(ways):
        refs[way][...] = total[pl.ds((along ^ way) * size, size)].astype(refs[way].dtype)


def last_kernel(ways, entry_ref, gain_ref, place_ref, low_ref, high_ref, own_ref, other_ref, out_ref, total, x):
    half = low_ref.shape[0]
    x[:half] = low_ref[...]
    x[half:] = high_ref[...]
    add_products(entry_ref, gain_ref, load_from(x), (own_ref, other_ref), total, True)
    along = place_ref[0]
    share = out_ref.shape[1]

    def write(group, carry):
        lanes = pl.ds(pl.multiple_of(group * LANES, LANES), LANES)
        values = total[group].astype(out_ref.dtype)
        for index in range(ways):
            out_ref[along ^ index, :, lanes] = values[index * share : (index + 1) * share]
        return carry

    lax.fori_loop(0, total.shape[0], write, 0)


def shards(strengths, blocks, pattern, level_gain):
    n_panel = lax.axis_size("panel")
    n_case = lax.axis_size("case")
    ways = n_panel // 2
    share, width = strengths.shape
    held_cases = share * ways
    slots = blocks.shape[0]
    col_blocks = width // B
    row_blocks = 2 * (col_blocks * n_case // n_panel)
    col_groups = col_blocks * PER
    row_groups = row_blocks * PER
    panel = lax.axis_index("panel")
    case = lax.axis_index("case")
    core = panel % 2
    along = panel // 2
    value = strengths.dtype

    strength_parts = [strengths] + [swap(strengths, "panel", 2 * way) for way in range(1, ways)]
    other_blocks = swap(blocks, "panel", 1)
    place = along.astype(jnp.int32)[None]
    first = jnp.stack([along * row_blocks, case * col_blocks, 0]).astype(jnp.int32)
    entry = jnp.where(pattern[:, 2:3] < 0, jnp.array([0, 0, -1], jnp.int32), pattern - first).reshape(-1)
    entry = jnp.concatenate([entry, swap(entry, "panel", 1)])

    smem = pl.BlockSpec(memory_space=pltpu.SMEM)
    vmem = pl.BlockSpec(memory_space=pltpu.VMEM)

    def product(kernel, small, vectors, outs, total_groups, x_groups):
        scratch = [pltpu.VMEM((total_groups, held_cases, LANES), jnp.float32)]
        if x_groups:
            scratch.append(pltpu.VMEM((x_groups, held_cases, LANES), value))
        return pl.pallas_call(
            kernel,
            out_shape=[jax.ShapeDtypeStruct(shape, value) for shape in outs],
            in_specs=[smem] * len(small) + [vmem] * (len(vectors) + 2),
            out_specs=[vmem] * len(outs),
            scratch_shapes=scratch,
            compiler_params=pltpu.CompilerParams(vmem_limit_bytes=VMEM_LIMIT),
            cost_estimate=pl.CostEstimate(
                flops=4 * held_cases * slots * B * B, bytes_accessed=4 * slots * B * B, transcendentals=0
            ),
        )(*small, *vectors, blocks, other_blocks)

    half_rows = [(row_groups // 2, held_cases, LANES)] * 2
    part_size = col_groups // ways

    def over_case(low, high):
        bits = [1 << b for b in range(n_case.bit_length() - 1)]
        for one, other in zip(bits, reversed(bits)):
            low_in, high_in = swap(low, "case", one), swap(high, "case", other)
            low, high = add_up(low, low_in), add_up(high, high_in)
        return low, high

    def scatter_along(parts):
        return add_up(parts[0], *[swap(parts[way], "panel", 2 * way) for way in range(1, ways)])

    def gather_along(part):
        return [part] + [swap(part, "panel", 2 * way) for way in range(1, ways)]

    def own_rows(low, high):
        count = held_cases // n_case
        mine, theirs = jnp.where(core == 0, low, high), jnp.where(core == 0, high, low)
        mine = lax.dynamic_slice_in_dim(mine, case * count, count, 1)
        theirs = swap(lax.dynamic_slice_in_dim(theirs, case * count, count, 1), "panel", 1)
        both = jnp.stack([jnp.where(core == 0, mine, theirs), jnp.where(core == 0, theirs, mine)])
        both = both.reshape(2, row_groups // 2, count // share, share, LANES)
        return jnp.transpose(both, (2, 0, 3, 1, 4)).reshape(2 * count, row_groups // 2 * LANES)

    def own_share(pieces):
        own = jnp.stack([lax.dynamic_slice_in_dim(one, along * share, share, 1) for one in pieces])
        bit = 1
        while bit < ways:
            flipped = own.reshape(ways // (2 * bit), 2, bit, part_size, share, LANES)[:, ::-1].reshape(own.shape)
            own = jnp.where(along & bit != 0, flipped, own)
            bit *= 2
        return jnp.moveaxis(own, 2, 0).reshape(share, width)

    stacked = jnp.zeros((ways, share, width), value)
    for way, one in enumerate(strength_parts):
        stacked = lax.dynamic_update_slice_in_dim(stacked, one[None], along ^ way, 0)
    low, high = product(first_kernel, (entry, level_gain), [stacked.reshape(held_cases, width)], half_rows, row_groups, 0)
    low, high = over_case(low, high)
    forward_one = own_rows(low, high)

    parts = product(
        functools.partial(adjoint_kernel, ways),
        (entry, level_gain, place),
        [low, high],
        [(part_size, held_cases, LANES)] * ways,
        col_groups,
        row_groups,
    )
    pieces = gather_along(scatter_along(parts))
    adjoint_one = own_share(pieces)

    low, high = product(
        functools.partial(forward_kernel, ways), (entry, level_gain, place), pieces, half_rows, row_groups, col_groups
    )
    low, high = over_case(low, high)
    forward_two = own_rows(low, high)

    (by_share,) = product(
        functools.partial(last_kernel, ways),
        (entry, level_gain, place),
        [low, high],
        [(ways, share, width)],
        col_groups,
        row_groups,
    )
    adjoint_two = scatter_along(by_share)
    return (forward_one, adjoint_one, forward_two, adjoint_two)


def solution(mesh):
    in_specs = (
        P("panel", "case"),
        P(("panel", "case"), None, None),
        P(("panel", "case"), None),
        P(),
    )
    out_specs = (P("case", "panel"), P("panel", "case"), P("case", "panel"), P("panel", "case"))
    return jax.shard_map(shards, mesh=mesh, in_specs=in_specs, out_specs=out_specs, check_vma=False)
```

```python
import functools

import jax
import jax.numpy as jnp
from jax import lax
from jax.experimental import pallas as pl
from jax.experimental.pallas import tpu as pltpu
from jax.sharding import PartitionSpec as P

B = 256
LANES = 128
PER = B // LANES
VMEM_LIMIT = 24 * 1024 * 1024


def swap(value, axis, offset, only=None):
    count = lax.axis_size(axis)
    pairs = [(i, i ^ offset) for i in range(count) if only is None or i % 2 == only]
    return lax.ppermute(value, axis, pairs)


def add_up(*parts):
    total = parts[0].astype(jnp.float32)
    for part in parts[1:]:
        total = total + part.astype(jnp.float32)
    return total.astype(parts[0].dtype)


def add_products(entry_ref, gain_ref, load, block_refs, total, adjoint):
    at = 0
    for block_ref in block_refs:
        for slot in range(block_ref.shape[0]):
            row, col, level = entry_ref[at], entry_ref[at + 1], entry_ref[at + 2]
            at += 3
            scale = jnp.where(level >= 0, gain_ref[jnp.maximum(level, 0)], jnp.float32(0.0))
            source, target = (row, col) if adjoint else (col, row)
            term = lax.dot_general(
                load(source),
                block_ref[slot],
                (((1,), (0 if adjoint else 1,)), ((), ())),
                preferred_element_type=jnp.float32,
            )
            term = term * scale
            for piece in range(PER):
                total[target * PER + piece] += term[:, piece * LANES : (piece + 1) * LANES]


def load_from(x):
    def load(block):
        return jnp.concatenate([x[block * PER + piece] for piece in range(PER)], axis=1)

    return load


def gate_kernel(value_ref, after_ref, out_ref):
    out_ref[...] = value_ref[...]


def first_kernel(entry_ref, gain_ref, x_ref, *refs):
    block_refs, (out_ref, total) = refs[:2], refs[-2:]
    total[...] = jnp.zeros_like(total)

    def load(block):
        return x_ref[:, pl.ds(pl.multiple_of(block * B, B), B)]

    add_products(entry_ref, gain_ref, load, block_refs, total, False)
    out_ref[...] = total[...].astype(out_ref.dtype)


def forward_kernel(ways, entry_ref, gain_ref, place_ref, *refs):
    pieces = refs[:ways]
    block_refs, (out_ref, total, x) = refs[ways : ways + 2], refs[-3:]
    total[...] = jnp.zeros_like(total)
    along = place_ref[0]
    size = pieces[0].shape[0]
    for way in range(ways):
        x[pl.ds((along ^ way) * size, size)] = pieces[way][...]
    add_products(entry_ref, gain_ref, load_from(x), block_refs, total, False)
    out_ref[...] = total[...].astype(out_ref.dtype)


def add_adjoint(entry_refs, gain_ref, own_x, other_x, block_refs, total):
    total[...] = jnp.zeros_like(total)
    add_products(entry_refs[0], gain_ref, load_from(own_x), block_refs[:2], total, True)
    add_products(entry_refs[1], gain_ref, load_from(other_x), block_refs[2:], total, True)


def adjoint_kernel(ways, own_entry, other_entry, gain_ref, place_ref, own_x, other_x, *refs):
    *block_refs, total = refs[:-ways - 1] + refs[-1:]
    outs = refs[-ways - 1 : -1]
    add_adjoint((own_entry, other_entry), gain_ref, own_x, other_x, block_refs, total)
    along = place_ref[0]
    size = outs[0].shape[0]
    for way in range(ways):
        outs[way][...] = total[pl.ds((along ^ way) * size, size)].astype(outs[way].dtype)


def last_kernel(kept, own_entry, other_entry, gain_ref, place_ref, own_x, other_x, *refs):
    total, out_ref = refs[-1], refs[-2 - kept]
    block_refs = refs[: -2 - 2 * kept]
    add_adjoint((own_entry, other_entry), gain_ref, own_x, other_x, block_refs, total)
    along = place_ref[0]
    ways, share, _ = out_ref.shape
    for group in range(total.shape[0]):
        values = total[group].astype(out_ref.dtype)
        for index in range(ways):
            out_ref[along ^ index, :, group * LANES : (group + 1) * LANES] = values[index * share : (index + 1) * share]


def shards(strengths, blocks, pattern, level_gain):
    n_panel = lax.axis_size("panel")
    n_case = lax.axis_size("case")
    ways = n_panel // 2
    share, width = strengths.shape
    held_cases = share * ways
    slots = blocks.shape[0]
    col_blocks = width // B
    row_blocks = col_blocks * n_case // n_panel
    col_groups = col_blocks * PER
    row_groups = row_blocks * PER
    part_size = col_groups // ways
    panel = lax.axis_index("panel")
    case = lax.axis_index("case")
    core = panel % 2
    along = panel // 2
    value = strengths.dtype

    smem = pl.BlockSpec(memory_space=pltpu.SMEM)
    vmem = pl.BlockSpec(memory_space=pltpu.VMEM)
    anywhere = pl.BlockSpec(memory_space=pl.ANY)
    params = pltpu.CompilerParams(vmem_limit_bytes=VMEM_LIMIT)

    def like(shape):
        return jax.ShapeDtypeStruct(shape, value)

    own_blocks = [blocks[: slots // 2], blocks[slots // 2 :]]
    other_blocks = [swap(part, "panel", 1) for part in own_blocks]
    early = [swap(strengths, "panel", 2 * way, 0) for way in range(1, ways)]
    later_strengths = pl.pallas_call(
        gate_kernel,
        out_shape=like(strengths.shape),
        in_specs=[vmem, anywhere],
        out_specs=vmem,
        compiler_params=params,
    )(strengths, other_blocks[0])
    late = [swap(later_strengths, "panel", 2 * way, 1) for way in range(1, ways)]
    place = along.astype(jnp.int32)[None]
    first = jnp.stack([panel * row_blocks, case * col_blocks, 0]).astype(jnp.int32)
    own_entry = jnp.where(pattern[:, 2:3] < 0, jnp.array([0, 0, -1], jnp.int32), pattern - first).reshape(-1)
    other_entry = swap(own_entry, "panel", 1)

    def product(kernel, small, vectors, parts, outs, total_groups, x_groups=0, kept=(), after=()):
        scratch = [pltpu.VMEM((total_groups, held_cases, LANES), jnp.float32)]
        if x_groups:
            scratch.append(pltpu.VMEM((x_groups, held_cases, LANES), value))
        held = sum(part.shape[0] for part in parts)
        before = len(small) + len(vectors) + len(parts)
        return pl.pallas_call(
            kernel,
            out_shape=[like(shape) for shape in outs] + [like(one.shape) for one in kept],
            in_specs=[smem] * len(small) + [vmem] * (len(vectors) + len(parts)) + [anywhere] * (len(kept) + len(after)),
            out_specs=[vmem] * len(outs) + [anywhere] * len(kept),
            scratch_shapes=scratch,
            input_output_aliases={before + i: len(outs) + i for i in range(len(kept))},
            compiler_params=params,
            cost_estimate=pl.CostEstimate(
                flops=2 * held_cases * held * B * B, bytes_accessed=2 * held * B * B, transcendentals=0
            ),
        )(*small, *vectors, *parts, *kept, *after)

    rows_shape = (row_groups, held_cases, LANES)

    def over_case(own, other):
        bits = [1 << b for b in range(n_case.bit_length() - 1)]
        for one, two in zip(bits, reversed(bits)):
            own_in, other_in = swap(own, "case", one), swap(other, "case", two)
            own, other = add_up(own, own_in), add_up(other, other_in)
        return own, other

    def scatter_along(parts):
        return add_up(parts[0], *[swap(parts[way], "panel", 2 * way) for way in range(1, ways)])

    def gather_along(part):
        return [part] + [swap(part, "panel", 2 * way) for way in range(1, ways)]

    def first_forward(x):
        (own,) = product(first_kernel, (own_entry, level_gain), [x], own_blocks, [rows_shape], row_groups)
        (other,) = product(
            first_kernel, (other_entry, level_gain), [x], other_blocks, [rows_shape], row_groups, after=[own]
        )
        return own, other

    def forward(pieces):
        kernel = functools.partial(forward_kernel, ways)
        (own,) = product(kernel, (own_entry, level_gain, place), pieces, own_blocks, [rows_shape], row_groups, col_groups)
        (other,) = product(
            kernel, (other_entry, level_gain, place), pieces, other_blocks, [rows_shape], row_groups, col_groups, after=[own]
        )
        return own, other

    def adjoint(kernel, own, other, outs, kept=()):
        small = (own_entry, other_entry, level_gain, place)
        return product(kernel, small, [own, other], [*own_blocks, *other_blocks], outs, col_groups, kept=kept)

    def own_rows(own, other):
        count = held_cases // n_case
        mine = lax.dynamic_slice_in_dim(own, case * count, count, 1)
        theirs = swap(lax.dynamic_slice_in_dim(other, case * count, count, 1), "panel", 1)
        both = jnp.stack([jnp.where(core == 0, mine, theirs), jnp.where(core == 0, theirs, mine)])
        both = both.reshape(2, row_groups, count // share, share, LANES)
        return jnp.transpose(both, (2, 0, 3, 1, 4)).reshape(2 * count, row_groups * LANES)

    def own_share(pieces):
        own = jnp.stack([lax.dynamic_slice_in_dim(one, along * share, share, 1) for one in pieces])
        bit = 1
        while bit < ways:
            flipped = own.reshape(ways // (2 * bit), 2, bit, part_size, share, LANES)[:, ::-1].reshape(own.shape)
            own = jnp.where(along & bit != 0, flipped, own)
            bit *= 2
        return jnp.moveaxis(own, 2, 0).reshape(share, width)

    stacked = jnp.zeros((ways, share, width), value)
    stacked = lax.dynamic_update_slice_in_dim(stacked, strengths[None], along, 0)
    for way in range(1, ways):
        one = jnp.where(core == 0, early[way - 1], late[way - 1])
        stacked = lax.dynamic_update_slice_in_dim(stacked, one[None], along ^ way, 0)
    first_sums = over_case(*first_forward(stacked.reshape(held_cases, width)))

    parts = adjoint(
        functools.partial(adjoint_kernel, ways), *first_sums, [(part_size, held_cases, LANES)] * ways
    )
    pieces = gather_along(scatter_along(parts))

    second_sums = over_case(*forward(pieces))
    kept = [*first_sums, *pieces]
    by_share, *kept = adjoint(
        functools.partial(last_kernel, len(kept)), *second_sums, [(ways, share, width)], kept
    )
    adjoint_two = scatter_along(by_share)
    forward_one = own_rows(*kept[:2])
    forward_two = own_rows(*second_sums)
    adjoint_one = own_share(kept[2:])
    return (forward_one, adjoint_one, forward_two, adjoint_two)


def solution(mesh):
    in_specs = (
        P("panel", "case"),
        P(("panel", "case"), None, None),
        P(("panel", "case"), None),
        P(),
    )
    out_specs = (P("case", "panel"), P("panel", "case"), P("case", "panel"), P("panel", "case"))
    return jax.shard_map(shards, mesh=mesh, in_specs=in_specs, out_specs=out_specs, check_vma=False)
```

```python
import functools

import jax
import jax.numpy as jnp
from jax import lax
from jax.experimental import pallas as pl
from jax.experimental.pallas import tpu as pltpu
from jax.sharding import PartitionSpec as P

B = 256
LANES = 128
PER = B // LANES
HELD_PARTS = 2
ROW_PARTS = 4
COL_PARTS = 2
VMEM_LIMIT = 24 * 1024 * 1024


def swap(value, axis, offset):
    count = lax.axis_size(axis)
    return lax.ppermute(value, axis, [(i, i ^ offset) for i in range(count)])


def add_up(*parts):
    total = parts[0].astype(jnp.float32)
    for part in parts[1:]:
        total = total + part.astype(jnp.float32)
    return total.astype(parts[0].dtype)


def spans(size, count):
    edges = [size * i // count for i in range(count + 1)]
    return [(a, b - a) for a, b in zip(edges, edges[1:])]


def add_products(entry_ref, gain_ref, load, block_refs, total, adjoint):
    total[...] = jnp.zeros_like(total)
    at = 0
    for block_ref in block_refs:
        for slot in range(block_ref.shape[0]):
            row, col, level = entry_ref[at], entry_ref[at + 1], entry_ref[at + 2]
            at += 3
            scale = jnp.where(level >= 0, gain_ref[jnp.maximum(level, 0)], jnp.float32(0.0))
            source, target = (row, col) if adjoint else (col, row)
            term = lax.dot_general(
                load(source),
                block_ref[slot],
                (((1,), (0 if adjoint else 1,)), ((), ())),
                preferred_element_type=jnp.float32,
            )
            term = term * scale
            for piece in range(PER):
                total[target * PER + piece] += term[:, piece * LANES : (piece + 1) * LANES]


def load_from(x):
    def load(block):
        return jnp.concatenate([x[block * PER + piece] for piece in range(PER)], axis=1)

    return load


def write_parts(total, outs):
    at = 0
    for out_ref in outs:
        size = out_ref.shape[0]
        out_ref[...] = total[at : at + size].astype(out_ref.dtype)
        at += size


def join_parts(x, parts):
    at = 0
    for part in parts:
        size = part.shape[0]
        x[at : at + size] = part[...]
        at += size


def first_kernel(entry_ref, gain_ref, x_ref, *refs):
    block_refs, outs, total = refs[:HELD_PARTS], refs[HELD_PARTS:-1], refs[-1]

    def load(block):
        return x_ref[:, pl.ds(pl.multiple_of(block * B, B), B)]

    add_products(entry_ref, gain_ref, load, block_refs, total, False)
    write_parts(total, outs)


def forward_kernel(ways, cuts, entry_ref, gain_ref, place_ref, *refs):
    count = len(cuts) * 2 * ways
    pieces, block_refs, outs = refs[:count], refs[count : count + HELD_PARTS], refs[count + HELD_PARTS : -2]
    total, x = refs[-2:]
    core, along = place_ref[0], place_ref[1]
    whole = sum(size for _, size in cuts)
    for cut, (start, size) in enumerate(cuts):
        for side in range(2):
            for way in range(ways):
                at = ((core ^ side) * ways + (along ^ way)) * whole + start
                x[pl.ds(at, size)] = pieces[(cut * 2 + side) * ways + way][...]
    add_products(entry_ref, gain_ref, load_from(x), block_refs, total, False)
    write_parts(total, outs)


def adjoint_kernel(ways, cuts, entry_ref, gain_ref, place_ref, *refs):
    parts, block_refs = refs[:ROW_PARTS], refs[ROW_PARTS : ROW_PARTS + HELD_PARTS]
    outs = refs[ROW_PARTS + HELD_PARTS : -2]
    total, x = refs[-2:]
    join_parts(x, parts)
    add_products(entry_ref, gain_ref, load_from(x), block_refs, total, True)
    core, along = place_ref[0], place_ref[1]
    whole = sum(size for _, size in cuts)
    for cut, (start, size) in enumerate(cuts):
        for side in range(2):
            out_ref = outs[cut * 2 + side]
            for way in range(ways):
                at = ((core ^ side) * ways + (along ^ way)) * whole + start
                out_ref[way] = total[pl.ds(at, size)].astype(out_ref.dtype)


def last_kernel(entry_ref, gain_ref, place_ref, *refs):
    parts, block_refs = refs[:ROW_PARTS], refs[ROW_PARTS : ROW_PARTS + HELD_PARTS]
    total, x = refs[-2:]
    kept = (len(refs) - 2 - ROW_PARTS - HELD_PARTS - COL_PARTS) // 2
    outs = refs[ROW_PARTS + HELD_PARTS + kept :][:COL_PARTS]
    join_parts(x, parts)
    add_products(entry_ref, gain_ref, load_from(x), block_refs, total, True)
    core, along = place_ref[0], place_ref[1]
    group = 0
    for out_ref in outs:
        _, ways, share, width = out_ref.shape
        for lane in range(0, width, LANES):
            values = total[group].astype(out_ref.dtype)
            group += 1
            for index in range(2 * ways):
                piece = values[index * share : (index + 1) * share]
                out_ref[core ^ (index % 2), along ^ (index // 2), :, lane : lane + LANES] = piece


def shards(strengths, blocks, pattern, level_gain):
    n_panel = lax.axis_size("panel")
    n_case = lax.axis_size("case")
    ways = n_panel // 2
    share, width = strengths.shape
    cases = share * n_panel
    slots = blocks.shape[0]
    col_blocks = width // B
    row_blocks = col_blocks * n_case // n_panel
    col_groups = col_blocks * PER
    row_groups = row_blocks * PER
    panel = lax.axis_index("panel")
    case = lax.axis_index("case")
    core = panel % 2
    along = panel // 2
    value = strengths.dtype
    row_cuts = spans(row_groups, ROW_PARTS)
    cuts = spans(col_groups // n_panel, COL_PARTS)

    place = jnp.stack([core, along]).astype(jnp.int32)
    first = jnp.stack([panel * row_blocks, case * col_blocks, 0]).astype(jnp.int32)
    entry = jnp.where(pattern[:, 2:3] < 0, jnp.array([0, 0, -1], jnp.int32), pattern - first).reshape(-1)
    held = [blocks[a : a + n] for a, n in spans(slots, HELD_PARTS)]

    smem = pl.BlockSpec(memory_space=pltpu.SMEM)
    vmem = pl.BlockSpec(memory_space=pltpu.VMEM)
    anywhere = pl.BlockSpec(memory_space=pl.ANY)

    def product(kernel, small, vectors, outs, total_groups, x_groups=0, kept=()):
        scratch = [pltpu.VMEM((total_groups, cases, LANES), jnp.float32)]
        if x_groups:
            scratch.append(pltpu.VMEM((x_groups, cases, LANES), value))
        before = len(small) + len(vectors) + len(held)
        return pl.pallas_call(
            kernel,
            out_shape=[jax.ShapeDtypeStruct(shape, value) for shape in (*outs, *(one.shape for one in kept))],
            in_specs=[smem] * len(small) + [vmem] * (len(vectors) + len(held)) + [anywhere] * len(kept),
            out_specs=[vmem] * len(outs) + [anywhere] * len(kept),
            scratch_shapes=scratch,
            input_output_aliases={before + i: len(outs) + i for i in range(len(kept))},
            compiler_params=pltpu.CompilerParams(vmem_limit_bytes=VMEM_LIMIT),
            cost_estimate=pl.CostEstimate(
                flops=2 * cases * slots * B * B, bytes_accessed=2 * slots * B * B, transcendentals=0
            ),
        )(*small, *vectors, *held, *kept)

    row_shapes = [(size, cases, LANES) for _, size in row_cuts]

    def over_case(parts):
        bits = [1 << b for b in range(n_case.bit_length() - 1)]
        parts = list(parts)
        for step in range(len(bits)):
            arrived = [swap(part, "case", bits[(step + i) % len(bits)]) for i, part in enumerate(parts)]
            parts = [add_up(part, one) for part, one in zip(parts, arrived)]
        return parts

    def scatter_panel(mine, theirs):
        return scatter_along(add_up(mine, swap(theirs, "panel", 1)))

    def scatter_along(summed):
        return add_up(summed[0], *[swap(summed[way], "panel", 2 * way) for way in range(1, ways)])

    def gather_panel(part):
        same = [part] + [swap(part, "panel", 2 * way) for way in range(1, ways)]
        return same + [swap(one, "panel", 1) for one in same]

    def own_cases(parts):
        whole = jnp.concatenate(parts)
        own = lax.dynamic_slice_in_dim(whole, case * (cases // n_case), cases // n_case, 1)
        return jnp.swapaxes(own, 0, 1).reshape(cases // n_case, row_groups * LANES)

    def own_share(pieces):
        picked = [lax.dynamic_slice_in_dim(one, panel * share, share, 1) for one in pieces]
        count = 2 * ways
        joined = [jnp.concatenate([picked[cut * count + i] for cut in range(len(cuts))]) for i in range(count)]
        own = jnp.stack(joined).reshape(2, ways, col_groups // n_panel, share, LANES)
        own = jnp.where(core == 1, own[::-1], own)
        bit = 1
        while bit < ways:
            flipped = own.reshape(2, ways // (2 * bit), 2, bit, *own.shape[2:])[:, :, ::-1].reshape(own.shape)
            own = jnp.where(along & bit != 0, flipped, own)
            bit *= 2
        return jnp.moveaxis(own, 3, 0).reshape(share, width)

    same_first = [strengths] + [swap(strengths, "panel", 2 * way) for way in range(1, ways)]
    other_first = [swap(one, "panel", 1) for one in same_first]
    stacked = jnp.zeros((n_panel, share, width), value)
    for side, parts in enumerate((same_first, other_first)):
        for way, one in enumerate(parts):
            stacked = lax.dynamic_update_slice_in_dim(stacked, one[None], panel ^ (2 * way + side), 0)
    x = stacked.reshape(cases, width)
    first_sums = over_case(product(first_kernel, (entry, level_gain), [x], row_shapes, row_groups))

    small = (entry, level_gain, place)
    outs = [(ways, size, cases, LANES) for _, size in cuts for _ in range(2)]
    halves = product(functools.partial(adjoint_kernel, ways, cuts), small, first_sums, outs, col_groups, row_groups)
    pieces = []
    for part in [scatter_panel(*halves[2 * cut : 2 * cut + 2]) for cut in range(len(cuts))]:
        pieces += gather_panel(part)

    kernel = functools.partial(forward_kernel, ways, cuts)
    second_sums = over_case(product(kernel, small, pieces, row_shapes, row_groups, col_groups))

    outs = [(2, ways, share, width // COL_PARTS)] * COL_PARTS
    kept = [*first_sums, *pieces]
    result = product(last_kernel, small, second_sums, outs, col_groups, row_groups, kept)
    by_share, kept = result[:COL_PARTS], result[COL_PARTS:]
    summed = [add_up(one[0], swap(one[1], "panel", 1)) for one in by_share]
    summed, kept, second_sums = lax.optimization_barrier((summed, kept, second_sums))
    adjoint_two = jnp.concatenate([scatter_along(one) for one in summed], axis=1)
    forward_one = own_cases(kept[:ROW_PARTS])
    forward_two = own_cases(second_sums)
    adjoint_one = own_share(kept[ROW_PARTS:])
    return (forward_one, adjoint_one, forward_two, adjoint_two)


def solution(mesh):
    in_specs = (
        P("panel", "case"),
        P(("panel", "case"), None, None),
        P(("panel", "case"), None),
        P(),
    )
    out_specs = (P("case", "panel"), P("panel", "case"), P("case", "panel"), P("panel", "case"))
    return jax.shard_map(shards, mesh=mesh, in_specs=in_specs, out_specs=out_specs, check_vma=False)
```

```python
import functools

import jax
import jax.numpy as jnp
from jax import lax
from jax.experimental import pallas as pl
from jax.experimental.pallas import tpu as pltpu
from jax.sharding import PartitionSpec as P

B = 256
LANES = 128
PER = B // LANES
VMEM_LIMIT = 12 * 1024 * 1024
CHUNK = 1536


def swap(value, axis, offset, only=None):
    count = lax.axis_size(axis)
    pairs = [(i, i ^ offset) for i in range(count) if only is None or i % 2 == only]
    return lax.ppermute(value, axis, pairs)


def add_up(*parts):
    total = parts[0].astype(jnp.float32)
    for part in parts[1:]:
        total = total + part.astype(jnp.float32)
    return total.astype(parts[0].dtype)


def add_products(entry_ref, gain_ref, load, block_refs, add, adjoint):
    at = 0
    for block_ref in block_refs:
        for slot in range(block_ref.shape[0]):
            row, col, level = entry_ref[at], entry_ref[at + 1], entry_ref[at + 2]
            at += 3
            scale = jnp.where(level >= 0, gain_ref[jnp.maximum(level, 0)], jnp.float32(0.0))
            source, target = (row, col) if adjoint else (col, row)
            term = lax.dot_general(
                load(source),
                block_ref[slot],
                (((1,), (0 if adjoint else 1,)), ((), ())),
                preferred_element_type=jnp.float32,
            )
            term = term * scale
            for piece in range(PER):
                add[target * PER + piece] += term[:, piece * LANES : (piece + 1) * LANES]


def load_from(x):
    def load(block):
        return jnp.concatenate([x[block * PER + piece] for piece in range(PER)], axis=1)

    return load


def gate_kernel(value_ref, after_ref, out_ref):
    out_ref[...] = value_ref[...]


def add_forward(own_entry, other_entry, gain_ref, load, block_refs, outs, totals):
    for total in totals:
        total[...] = jnp.zeros_like(total)
    add_products(own_entry, gain_ref, load, block_refs[:2], totals[0], False)
    add_products(other_entry, gain_ref, load, block_refs[2:], totals[1], False)
    for out_ref, total in zip(outs, totals):
        out_ref[...] = total[...].astype(out_ref.dtype)


def first_kernel(ways, own_entry, other_entry, gain_ref, place_ref, mine_ref, *refs):
    early, late = refs[: ways - 1], refs[ways - 1 : 2 * ways - 2]
    *block_refs, own_out, other_out, own_total, other_total, wide, x = refs[2 * ways - 2 :]
    along, is_even = place_ref[0], place_ref[1] == 0
    share, width = mine_ref.shape
    for start in range(0, width, CHUNK):
        lanes = slice(start, min(start + CHUNK, width))
        rows = [mine_ref[:, lanes].astype(jnp.float32)]
        for a, b in zip(early, late):
            rows.append(jnp.where(is_even, a[:, lanes].astype(jnp.float32), b[:, lanes].astype(jnp.float32)))
        bit = 1
        while bit < ways:
            flip = (along & bit) != 0
            rows = [jnp.where(flip, rows[i ^ bit], rows[i]) for i in range(ways)]
            bit *= 2
        for i, row in enumerate(rows):
            wide[i * share : (i + 1) * share, lanes] = row
        x[:, lanes] = wide[:, lanes].astype(x.dtype)

    def load(block):
        return x[:, pl.ds(pl.multiple_of(block * B, B), B)]

    outs, totals = (own_out, other_out), (own_total, other_total)
    add_forward(own_entry, other_entry, gain_ref, load, block_refs, outs, totals)


def forward_kernel(ways, own_entry, other_entry, gain_ref, place_ref, *refs):
    pieces = refs[:ways]
    *block_refs, own_out, other_out, own_total, other_total, x = refs[ways:]
    along = place_ref[0]
    size = pieces[0].shape[0]
    for way in range(ways):
        x[pl.ds((along ^ way) * size, size)] = pieces[way][...]
    outs, totals = (own_out, other_out), (own_total, other_total)
    add_forward(own_entry, other_entry, gain_ref, load_from(x), block_refs, outs, totals)


def add_adjoint(entry_refs, gain_ref, own_x, other_x, block_refs, total):
    total[...] = jnp.zeros_like(total)
    add_products(entry_refs[0], gain_ref, load_from(own_x), block_refs[:2], total, True)
    add_products(entry_refs[1], gain_ref, load_from(other_x), block_refs[2:], total, True)


def adjoint_kernel(ways, own_entry, other_entry, gain_ref, place_ref, own_x, other_x, *refs):
    block_refs, total = refs[: -ways - 1], refs[-1]
    outs = refs[-ways - 1 : -1]
    add_adjoint((own_entry, other_entry), gain_ref, own_x, other_x, block_refs, total)
    along = place_ref[0]
    size = outs[0].shape[0]
    for way in range(ways):
        outs[way][...] = total[pl.ds((along ^ way) * size, size)].astype(outs[way].dtype)


def last_kernel(ways, own_entry, other_entry, gain_ref, place_ref, own_x, other_x, *refs):
    block_refs, total = refs[:3], refs[-1]
    out_ref = refs[3 + (len(refs) - 5) // 2]
    add_adjoint((own_entry, other_entry), gain_ref, own_x, other_x, block_refs, total)
    along = place_ref[0]
    share = out_ref.shape[1]
    for group in range(total.shape[0]):
        values = total[group].astype(out_ref.dtype)
        for index in range(ways):
            out_ref[along ^ index, :, group * LANES : (group + 1) * LANES] = values[index * share : (index + 1) * share]


def shards(strengths, blocks, pattern, level_gain):
    n_panel = lax.axis_size("panel")
    n_case = lax.axis_size("case")
    ways = n_panel // 2
    share, width = strengths.shape
    held_cases = share * ways
    slots = blocks.shape[0]
    col_blocks = width // B
    row_blocks = col_blocks * n_case // n_panel
    col_groups = col_blocks * PER
    row_groups = row_blocks * PER
    part_size = col_groups // ways
    panel = lax.axis_index("panel")
    case = lax.axis_index("case")
    core = panel % 2
    along = panel // 2
    value = strengths.dtype

    smem = pl.BlockSpec(memory_space=pltpu.SMEM)
    vmem = pl.BlockSpec(memory_space=pltpu.VMEM)
    anywhere = pl.BlockSpec(memory_space=pl.ANY)
    params = pltpu.CompilerParams(vmem_limit_bytes=VMEM_LIMIT)

    def like(shape):
        return jax.ShapeDtypeStruct(shape, value)

    place = jnp.stack([along, core]).astype(jnp.int32)
    first = jnp.stack([panel * row_blocks, case * col_blocks, 0]).astype(jnp.int32)
    own_entry = jnp.where(pattern[:, 2:3] < 0, jnp.array([0, 0, -1], jnp.int32), pattern - first).reshape(-1)
    early = [swap(strengths, "panel", 2 * way, 0) for way in range(1, ways)]
    other_entry = swap(own_entry, "panel", 1)
    other_blocks = swap(lax.optimization_barrier((blocks, other_entry))[0], "panel", 1)
    later_strengths = pl.pallas_call(
        gate_kernel,
        out_shape=like(strengths.shape),
        in_specs=[vmem, anywhere],
        out_specs=vmem,
        compiler_params=params,
    )(strengths, other_entry)
    late = [swap(later_strengths, "panel", 2 * way, 1) for way in range(1, ways)]
    later_blocks = lax.optimization_barrier((blocks, later_strengths))[0]
    own_blocks = [later_blocks[: slots // 2], later_blocks[slots // 2 :]]

    def product(kernel, vectors, outs, scratch, kept=()):
        small = (own_entry, other_entry, level_gain, place)
        parts = (*own_blocks, other_blocks)
        before = len(small) + len(vectors) + len(parts)
        return pl.pallas_call(
            functools.partial(kernel, ways),
            out_shape=[like(shape) for shape in outs] + [like(one.shape) for one in kept],
            in_specs=[smem] * len(small) + [vmem] * (len(vectors) + len(parts)) + [anywhere] * len(kept),
            out_specs=[vmem] * len(outs) + [anywhere] * len(kept),
            scratch_shapes=scratch,
            input_output_aliases={before + i: len(outs) + i for i in range(len(kept))},
            compiler_params=params,
            cost_estimate=pl.CostEstimate(
                flops=4 * held_cases * slots * B * B, bytes_accessed=4 * slots * B * B, transcendentals=0
            ),
        )(*small, *vectors, *parts, *kept)

    rows_total = pltpu.VMEM((row_groups, held_cases, LANES), jnp.float32)
    cols_total = pltpu.VMEM((col_groups, held_cases, LANES), jnp.float32)
    cols_held = pltpu.VMEM((col_groups, held_cases, LANES), value)
    rows_shape = (row_groups, held_cases, LANES)

    def over_case(own, other):
        bits = [1 << b for b in range(n_case.bit_length() - 1)]
        for one, two in zip(bits, reversed(bits)):
            own_in, other_in = swap(own, "case", one), swap(other, "case", two)
            own, other = add_up(own, own_in), add_up(other, other_in)
        return own, other

    def scatter_along(parts):
        return add_up(parts[0], *[swap(parts[way], "panel", 2 * way) for way in range(1, ways)])

    def gather_along(part):
        return [part] + [swap(part, "panel", 2 * way) for way in range(1, ways)]

    def own_rows(own, other):
        count = held_cases // n_case
        mine = lax.dynamic_slice_in_dim(own, case * count, count, 1)
        theirs = swap(lax.dynamic_slice_in_dim(other, case * count, count, 1), "panel", 1)
        both = jnp.stack([jnp.where(core == 0, mine, theirs), jnp.where(core == 0, theirs, mine)])
        both = both.reshape(2, row_groups, count // share, share, LANES)
        return jnp.transpose(both, (2, 0, 3, 1, 4)).reshape(2 * count, row_groups * LANES)

    def own_share(pieces):
        own = jnp.stack([lax.dynamic_slice_in_dim(one, along * share, share, 1) for one in pieces])
        bit = 1
        while bit < ways:
            flipped = own.reshape(ways // (2 * bit), 2, bit, part_size, share, LANES)[:, ::-1].reshape(own.shape)
            own = jnp.where(along & bit != 0, flipped, own)
            bit *= 2
        return jnp.moveaxis(own, 2, 0).reshape(share, width)

    flat = [pltpu.VMEM((held_cases, width), kind) for kind in (jnp.float32, value)]
    sums = product(first_kernel, [strengths, *early, *late], [rows_shape] * 2, [rows_total] * 2 + flat)
    first_sums = over_case(*sums)

    parts = product(adjoint_kernel, first_sums, [(part_size, held_cases, LANES)] * ways, [cols_total])
    pieces = gather_along(scatter_along(parts))

    sums = product(forward_kernel, pieces, [rows_shape] * 2, [rows_total] * 2 + [cols_held])
    second_sums = over_case(*sums)
    kept = [*first_sums, *pieces]
    by_share, *kept = product(last_kernel, second_sums, [(ways, share, width)], [cols_total], kept)
    adjoint_two = scatter_along(by_share)
    forward_one = own_rows(*kept[:2])
    forward_two = own_rows(*second_sums)
    adjoint_one = own_share(kept[2:])
    return (forward_one, adjoint_one, forward_two, adjoint_two)


def solution(mesh):
    in_specs = (
        P("panel", "case"),
        P(("panel", "case"), None, None),
        P(("panel", "case"), None),
        P(),
    )
    out_specs = (P("case", "panel"), P("panel", "case"), P("case", "panel"), P("panel", "case"))
    return jax.shard_map(shards, mesh=mesh, in_specs=in_specs, out_specs=out_specs, check_vma=False)
```

```python
import functools
import math

import jax
import jax.numpy as jnp
from jax import lax
from jax.experimental import pallas as pl
from jax.experimental.pallas import tpu as pltpu
from jax.sharding import PartitionSpec as P

B = 256
LANES = 128
PER = B // LANES
HELD_PARTS = 2
ROW_PARTS = 2
CHUNK = 1536
VMEM_LIMIT = 12 * 1024 * 1024


def swap(value, axis, offset):
    count = lax.axis_size(axis)
    return lax.ppermute(value, axis, [(i, i ^ offset) for i in range(count)])


def add_up(*parts):
    total = parts[0].astype(jnp.float32)
    for part in parts[1:]:
        total = total + part.astype(jnp.float32)
    return total.astype(parts[0].dtype)


def spans(size, count):
    edges = [size * i // count for i in range(count + 1)]
    return [(a, b - a) for a, b in zip(edges, edges[1:])]


def add_products(entry_ref, gain_ref, load, block_refs, total, adjoint):
    total[...] = jnp.zeros_like(total)
    at = 0
    for block_ref in block_refs:
        for slot in range(block_ref.shape[0]):
            row, col, level = entry_ref[at], entry_ref[at + 1], entry_ref[at + 2]
            at += 3
            scale = jnp.where(level >= 0, gain_ref[jnp.maximum(level, 0)], jnp.float32(0.0))
            source, target = (row, col) if adjoint else (col, row)
            term = lax.dot_general(
                load(source),
                block_ref[slot],
                (((1,), (0 if adjoint else 1,)), ((), ())),
                preferred_element_type=jnp.float32,
            )
            term = term * scale
            for piece in range(PER):
                total[target * PER + piece] += term[:, piece * LANES : (piece + 1) * LANES]


def load_from(x):
    def load(block):
        return jnp.concatenate([x[block * PER + piece] for piece in range(PER)], axis=1)

    return load


def write_parts(total, outs):
    at = 0
    for out_ref in outs:
        size = out_ref.shape[0]
        out_ref[...] = total[at : at + size].astype(out_ref.dtype)
        at += size


def join_parts(x, parts):
    at = 0
    for part in parts:
        size = part.shape[0]
        x[at : at + size] = part[...]
        at += size


def first_kernel(ways, entry_ref, gain_ref, place_ref, *refs):
    count = 2 * ways
    pieces, block_refs, outs = refs[:count], refs[count : count + HELD_PARTS], refs[count + HELD_PARTS : -3]
    total, wide, x = refs[-3:]
    core, along = place_ref[0], place_ref[1]
    share, width = pieces[0].shape
    chunk = math.gcd(width, CHUNK)

    def assemble(step, carry):
        lanes = pl.ds(pl.multiple_of(step * chunk, chunk), chunk)
        rows = [piece[:, lanes].astype(jnp.float32) for piece in pieces]
        bit, place = 1, along + core * ways
        while bit < count:
            flip = (place & bit) != 0
            rows = [jnp.where(flip, rows[i ^ bit], rows[i]) for i in range(count)]
            bit *= 2
        for side in range(2):
            for way in range(ways):
                at = (2 * way + side) * share
                wide[at : at + share, lanes] = rows[side * ways + way]
        x[:, lanes] = wide[:, lanes].astype(x.dtype)
        return carry

    lax.fori_loop(0, width // chunk, assemble, 0)

    def load(block):
        return x[:, pl.ds(pl.multiple_of(block * B, B), B)]

    add_products(entry_ref, gain_ref, load, block_refs, total, False)
    write_parts(total, outs)


def forward_kernel(ways, entry_ref, gain_ref, place_ref, *refs):
    count = 2 * ways
    pieces, block_refs, outs = refs[:count], refs[count : count + HELD_PARTS], refs[count + HELD_PARTS : -2]
    total, x = refs[-2:]
    core, along = place_ref[0], place_ref[1]
    size = pieces[0].shape[0]
    for side in range(2):
        for way in range(ways):
            at = ((core ^ side) * ways + (along ^ way)) * size
            x[pl.ds(at, size)] = pieces[side * ways + way][...]
    add_products(entry_ref, gain_ref, load_from(x), block_refs, total, False)
    write_parts(total, outs)


def adjoint_kernel(ways, entry_ref, gain_ref, place_ref, *refs):
    parts, block_refs = refs[:ROW_PARTS], refs[ROW_PARTS : ROW_PARTS + HELD_PARTS]
    outs = refs[ROW_PARTS + HELD_PARTS : -2]
    total, x = refs[-2:]
    join_parts(x, parts)
    add_products(entry_ref, gain_ref, load_from(x), block_refs, total, True)
    core, along = place_ref[0], place_ref[1]
    size = outs[0].shape[1]
    for side, out_ref in enumerate(outs):
        for way in range(ways):
            at = ((core ^ side) * ways + (along ^ way)) * size
            out_ref[way] = total[pl.ds(at, size)].astype(out_ref.dtype)


def last_kernel(ways, entry_ref, gain_ref, place_ref, *refs):
    parts, block_refs = refs[:ROW_PARTS], refs[ROW_PARTS : ROW_PARTS + HELD_PARTS]
    out_ref, total, x = refs[ROW_PARTS + HELD_PARTS :]
    join_parts(x, parts)
    add_products(entry_ref, gain_ref, load_from(x), block_refs, total, True)
    core, along = place_ref[0], place_ref[1]
    share = out_ref.shape[2]
    for group in range(total.shape[0]):
        values = total[group].astype(out_ref.dtype)
        for index in range(2 * ways):
            piece = values[index * share : (index + 1) * share]
            out_ref[core ^ (index % 2), along ^ (index // 2), :, group * LANES : (group + 1) * LANES] = piece


def shards(strengths, blocks, pattern, level_gain):
    n_panel = lax.axis_size("panel")
    n_case = lax.axis_size("case")
    ways = n_panel // 2
    share, width = strengths.shape
    cases = share * n_panel
    slots = blocks.shape[0]
    col_blocks = width // B
    row_blocks = col_blocks * n_case // n_panel
    col_groups = col_blocks * PER
    row_groups = row_blocks * PER
    panel = lax.axis_index("panel")
    case = lax.axis_index("case")
    core = panel % 2
    along = panel // 2
    value = strengths.dtype
    row_cuts = spans(row_groups, ROW_PARTS)
    part_size = col_groups // n_panel

    place = jnp.stack([core, along]).astype(jnp.int32)
    first = jnp.stack([panel * row_blocks, case * col_blocks, 0]).astype(jnp.int32)
    entry = jnp.where(pattern[:, 2:3] < 0, jnp.array([0, 0, -1], jnp.int32), pattern - first).reshape(-1)
    held = [blocks[a : a + n] for a, n in spans(slots, HELD_PARTS)]

    smem = pl.BlockSpec(memory_space=pltpu.SMEM)
    vmem = pl.BlockSpec(memory_space=pltpu.VMEM)

    def product(kernel, vectors, outs, scratch):
        small = (entry, level_gain, place)
        return pl.pallas_call(
            functools.partial(kernel, ways),
            out_shape=[jax.ShapeDtypeStruct(shape, value) for shape in outs],
            in_specs=[smem] * len(small) + [vmem] * (len(vectors) + len(held)),
            out_specs=[vmem] * len(outs),
            scratch_shapes=scratch,
            compiler_params=pltpu.CompilerParams(vmem_limit_bytes=VMEM_LIMIT),
            cost_estimate=pl.CostEstimate(
                flops=2 * cases * slots * B * B, bytes_accessed=2 * slots * B * B, transcendentals=0
            ),
        )(*small, *vectors, *held)

    def scratch(groups, kind):
        return pltpu.VMEM((groups, cases, LANES), kind)

    rows_total, rows_held = scratch(row_groups, jnp.float32), scratch(row_groups, value)
    cols_total, cols_held = scratch(col_groups, jnp.float32), scratch(col_groups, value)
    flat = [pltpu.VMEM((cases, width), kind) for kind in (jnp.float32, value)]
    row_shapes = [(size, cases, LANES) for _, size in row_cuts]

    def over_case(parts):
        bits = [1 << b for b in range(n_case.bit_length() - 1)]
        parts = list(parts)
        for step in range(len(bits)):
            arrived = [swap(part, "case", bits[(step + i) % len(bits)]) for i, part in enumerate(parts)]
            parts = [add_up(part, one) for part, one in zip(parts, arrived)]
        return parts

    def scatter_panel(mine, theirs):
        return scatter_along(add_up(mine, swap(theirs, "panel", 1)))

    def scatter_along(summed):
        return add_up(summed[0], *[swap(summed[way], "panel", 2 * way) for way in range(1, ways)])

    def gather_panel(part):
        same = [part] + [swap(part, "panel", 2 * way) for way in range(1, ways)]
        return same + [swap(one, "panel", 1) for one in same]

    def own_cases(parts):
        whole = jnp.concatenate(parts)
        own = lax.dynamic_slice_in_dim(whole, case * (cases // n_case), cases // n_case, 1)
        return jnp.swapaxes(own, 0, 1).reshape(cases // n_case, row_groups * LANES)

    def own_share(pieces):
        own = jnp.stack([lax.dynamic_slice_in_dim(one, panel * share, share, 1) for one in pieces])
        own = own.reshape(2, ways, part_size, share, LANES)
        own = jnp.where(core == 1, own[::-1], own)
        bit = 1
        while bit < ways:
            flipped = own.reshape(2, ways // (2 * bit), 2, bit, *own.shape[2:])[:, :, ::-1].reshape(own.shape)
            own = jnp.where(along & bit != 0, flipped, own)
            bit *= 2
        return jnp.moveaxis(own, 3, 0).reshape(share, width)

    first_sums = over_case(product(first_kernel, gather_panel(strengths), row_shapes, [rows_total, *flat]))
    outs = [(ways, part_size, cases, LANES)] * 2
    pieces = gather_panel(scatter_panel(*product(adjoint_kernel, first_sums, outs, [cols_total, rows_held])))
    second_sums = over_case(product(forward_kernel, pieces, row_shapes, [rows_total, cols_held]))
    (by_share,) = product(last_kernel, second_sums, [(2, ways, share, width)], [cols_total, rows_held])
    summed = add_up(by_share[0], swap(by_share[1], "panel", 1))

    summed, first_sums, pieces, second_sums = lax.optimization_barrier((summed, first_sums, pieces, second_sums))
    adjoint_two = scatter_along(summed)
    forward_one = own_cases(first_sums)
    forward_two = own_cases(second_sums)
    adjoint_one = own_share(pieces)
    return (forward_one, adjoint_one, forward_two, adjoint_two)


def solution(mesh):
    in_specs = (
        P("panel", "case"),
        P(("panel", "case"), None, None),
        P(("panel", "case"), None),
        P(),
    )
    out_specs = (P("case", "panel"), P("panel", "case"), P("case", "panel"), P("panel", "case"))
    return jax.shard_map(shards, mesh=mesh, in_specs=in_specs, out_specs=out_specs, check_vma=False)
```

```python
import functools
import math

import jax
import jax.numpy as jnp
from jax import lax
from jax.experimental import pallas as pl
from jax.experimental.pallas import tpu as pltpu
from jax.sharding import PartitionSpec as P

B = 256
LANES = 128
PER = B // LANES
COPIES = 4
ROW_PARTS = 2
CHUNK = 1536
VMEM_LIMIT = 12 * 1024 * 1024


def swap(value, axis, offset):
    count = lax.axis_size(axis)
    return lax.ppermute(value, axis, [(i, i ^ offset) for i in range(count)])


def add_up(*parts):
    total = parts[0].astype(jnp.float32)
    for part in parts[1:]:
        total = total + part.astype(jnp.float32)
    return total.astype(parts[0].dtype)


def spans(size, count):
    edges = [size * i // count for i in range(count + 1)]
    return [(a, b - a) for a, b in zip(edges, edges[1:])]


def hold_kernel(blocks_ref, held_ref, sems):
    copies = []
    for i, (start, size) in enumerate(spans(blocks_ref.shape[0], COPIES)):
        span = pl.ds(start, size)
        copies.append(pltpu.make_async_copy(blocks_ref.at[span], held_ref.at[span], sems.at[i]))
    for copy in copies:
        copy.start()
    for copy in copies:
        copy.wait()


def pick_rows(values, index, size):
    values = values.astype(jnp.float32)
    picked = values[:size]
    for i in range(1, values.shape[0] // size):
        picked = jnp.where(index == i, values[i * size : (i + 1) * size], picked)
    return picked


def cut_rows(place_ref, parts, out_ref):
    at = 0
    for part in parts:
        for group in range(part.shape[0]):
            picked = pick_rows(part[group], place_ref[2], out_ref.shape[0])
            out_ref[:, at : at + LANES] = picked.astype(out_ref.dtype)
            at += LANES


def cut_kernel(ways, place_ref, *refs):
    parts, pieces, (rows_ref, share_ref) = refs[:ROW_PARTS], refs[ROW_PARTS:-2], refs[-2:]
    cut_rows(place_ref, parts, rows_ref)
    core, along = place_ref[0], place_ref[1]
    panel = along * 2 + core
    for side in range(2):
        for way in range(ways):
            piece = pieces[side * ways + way]
            at = ((core ^ side) * ways + (along ^ way)) * piece.shape[0]
            for group in range(piece.shape[0]):
                lanes = pl.ds(pl.multiple_of((at + group) * LANES, LANES), LANES)
                picked = pick_rows(piece[group], panel, share_ref.shape[0])
                share_ref[:, lanes] = picked.astype(share_ref.dtype)


def cut_last_kernel(ways, place_ref, *refs):
    cut_rows(place_ref, refs[:-1], refs[-1])


def add_products(entry_ref, gain_ref, load, block_refs, total, adjoint):
    total[...] = jnp.zeros_like(total)
    at = 0
    for block_ref in block_refs:
        for slot in range(block_ref.shape[0]):
            row, col, level = entry_ref[at], entry_ref[at + 1], entry_ref[at + 2]
            at += 3
            scale = jnp.where(level >= 0, gain_ref[jnp.maximum(level, 0)], jnp.float32(0.0))
            source, target = (row, col) if adjoint else (col, row)
            term = lax.dot_general(
                load(source),
                block_ref[slot],
                (((1,), (0 if adjoint else 1,)), ((), ())),
                preferred_element_type=jnp.float32,
            )
            term = term * scale
            for piece in range(PER):
                total[target * PER + piece] += term[:, piece * LANES : (piece + 1) * LANES]


def load_from(x):
    def load(block):
        return jnp.concatenate([x[block * PER + piece] for piece in range(PER)], axis=1)

    return load


def write_parts(total, outs):
    at = 0
    for out_ref in outs:
        size = out_ref.shape[0]
        out_ref[...] = total[at : at + size].astype(out_ref.dtype)
        at += size


def join_parts(x, parts):
    at = 0
    for part in parts:
        size = part.shape[0]
        x[at : at + size] = part[...]
        at += size


def first_kernel(ways, entry_ref, gain_ref, place_ref, *refs):
    count = 2 * ways
    pieces, block_refs, outs = refs[:count], refs[count : count + 1], refs[count + 1 : -3]
    total, wide, x = refs[-3:]
    core, along = place_ref[0], place_ref[1]
    share, width = pieces[0].shape
    chunk = math.gcd(width, CHUNK)

    def assemble(step, carry):
        lanes = pl.ds(pl.multiple_of(step * chunk, chunk), chunk)
        rows = [piece[:, lanes].astype(jnp.float32) for piece in pieces]
        bit, place = 1, along + core * ways
        while bit < count:
            flip = (place & bit) != 0
            rows = [jnp.where(flip, rows[i ^ bit], rows[i]) for i in range(count)]
            bit *= 2
        for side in range(2):
            for way in range(ways):
                at = (2 * way + side) * share
                wide[at : at + share, lanes] = rows[side * ways + way]
        x[:, lanes] = wide[:, lanes].astype(x.dtype)
        return carry

    lax.fori_loop(0, width // chunk, assemble, 0)

    def load(block):
        return x[:, pl.ds(pl.multiple_of(block * B, B), B)]

    add_products(entry_ref, gain_ref, load, block_refs, total, False)
    write_parts(total, outs)


def forward_kernel(ways, entry_ref, gain_ref, place_ref, *refs):
    count = 2 * ways
    pieces, block_refs, outs = refs[:count], refs[count : count + 1], refs[count + 1 : -2]
    total, x = refs[-2:]
    core, along = place_ref[0], place_ref[1]
    size = pieces[0].shape[0]
    for side in range(2):
        for way in range(ways):
            at = ((core ^ side) * ways + (along ^ way)) * size
            x[pl.ds(at, size)] = pieces[side * ways + way][...]
    add_products(entry_ref, gain_ref, load_from(x), block_refs, total, False)
    write_parts(total, outs)


def adjoint_kernel(ways, entry_ref, gain_ref, place_ref, *refs):
    parts, block_refs = refs[:ROW_PARTS], refs[ROW_PARTS : ROW_PARTS + 1]
    outs = refs[ROW_PARTS + 1 : -2]
    total, x = refs[-2:]
    join_parts(x, parts)
    add_products(entry_ref, gain_ref, load_from(x), block_refs, total, True)
    core, along = place_ref[0], place_ref[1]
    size = outs[0].shape[1]
    for side, out_ref in enumerate(outs):
        for way in range(ways):
            at = ((core ^ side) * ways + (along ^ way)) * size
            out_ref[way] = total[pl.ds(at, size)].astype(out_ref.dtype)


def last_kernel(ways, entry_ref, gain_ref, place_ref, *refs):
    parts, block_refs = refs[:ROW_PARTS], refs[ROW_PARTS : ROW_PARTS + 1]
    out_ref, total, x = refs[ROW_PARTS + 1 :]
    join_parts(x, parts)
    add_products(entry_ref, gain_ref, load_from(x), block_refs, total, True)
    core, along = place_ref[0], place_ref[1]
    share = out_ref.shape[2]
    for group in range(total.shape[0]):
        values = total[group].astype(out_ref.dtype)
        for index in range(2 * ways):
            piece = values[index * share : (index + 1) * share]
            out_ref[core ^ (index % 2), along ^ (index // 2), :, group * LANES : (group + 1) * LANES] = piece


def shards(strengths, blocks, pattern, level_gain):
    n_panel = lax.axis_size("panel")
    n_case = lax.axis_size("case")
    ways = n_panel // 2
    share, width = strengths.shape
    cases = share * n_panel
    slots = blocks.shape[0]
    col_blocks = width // B
    row_blocks = col_blocks * n_case // n_panel
    col_groups = col_blocks * PER
    row_groups = row_blocks * PER
    panel = lax.axis_index("panel")
    case = lax.axis_index("case")
    core = panel % 2
    along = panel // 2
    value = strengths.dtype
    row_cuts = spans(row_groups, ROW_PARTS)
    part_size = col_groups // n_panel

    place = jnp.stack([core, along, case]).astype(jnp.int32)
    first = jnp.stack([panel * row_blocks, case * col_blocks, 0]).astype(jnp.int32)
    entry = jnp.where(pattern[:, 2:3] < 0, jnp.array([0, 0, -1], jnp.int32), pattern - first).reshape(-1)

    smem = pl.BlockSpec(memory_space=pltpu.SMEM)
    vmem = pl.BlockSpec(memory_space=pltpu.VMEM)

    params = pltpu.CompilerParams(vmem_limit_bytes=VMEM_LIMIT)
    held = pl.pallas_call(
        hold_kernel,
        out_shape=jax.ShapeDtypeStruct(blocks.shape, blocks.dtype),
        in_specs=[pl.BlockSpec(memory_space=pl.ANY)],
        out_specs=vmem,
        scratch_shapes=[pltpu.SemaphoreType.DMA((COPIES,))],
        compiler_params=params,
        cost_estimate=pl.CostEstimate(flops=0, bytes_accessed=2 * slots * B * B, transcendentals=0),
    )(blocks)

    def cut(kernel, vectors, outs):
        return pl.pallas_call(
            functools.partial(kernel, ways),
            out_shape=[jax.ShapeDtypeStruct(shape, value) for shape in outs],
            in_specs=[smem] + [vmem] * len(vectors),
            out_specs=[vmem] * len(outs),
            compiler_params=params,
            cost_estimate=pl.CostEstimate(flops=0, bytes_accessed=8 * share * width, transcendentals=0),
        )(place, *vectors)

    def product(kernel, vectors, outs, scratch):
        small = (entry, level_gain, place)
        return pl.pallas_call(
            functools.partial(kernel, ways),
            out_shape=[jax.ShapeDtypeStruct(shape, value) for shape in outs],
            in_specs=[smem] * len(small) + [vmem] * (len(vectors) + 1),
            out_specs=[vmem] * len(outs),
            scratch_shapes=scratch,
            compiler_params=params,
            cost_estimate=pl.CostEstimate(
                flops=2 * cases * slots * B * B, bytes_accessed=2 * slots * B * B, transcendentals=0
            ),
        )(*small, *vectors, held)

    def scratch(groups, kind):
        return pltpu.VMEM((groups, cases, LANES), kind)

    rows_total, rows_held = scratch(row_groups, jnp.float32), scratch(row_groups, value)
    cols_total, cols_held = scratch(col_groups, jnp.float32), scratch(col_groups, value)
    flat = [pltpu.VMEM((cases, width), kind) for kind in (jnp.float32, value)]
    row_shapes = [(size, cases, LANES) for _, size in row_cuts]

    def over_case(parts):
        bits = [1 << b for b in range(n_case.bit_length() - 1)]
        parts = list(parts)
        for step in range(len(bits)):
            arrived = [swap(part, "case", bits[(step + i) % len(bits)]) for i, part in enumerate(parts)]
            parts = [add_up(part, one) for part, one in zip(parts, arrived)]
        return parts

    def scatter_panel(mine, theirs):
        return scatter_along(add_up(mine, swap(theirs, "panel", 1)))

    far_first = sorted(range(1, ways), key=lambda way: way & (ways // 2) == 0)

    def along_swaps(part_of):
        arrived = {way: swap(part_of(way), "panel", 2 * way) for way in far_first}
        return [arrived[way] for way in range(1, ways)]

    def scatter_along(summed):
        return add_up(summed[0], *along_swaps(lambda way: summed[way]))

    def gather_panel(part):
        same = [part, *along_swaps(lambda way: part)]
        return same + [swap(one, "panel", 1) for one in same]

    first_sums = over_case(product(first_kernel, gather_panel(strengths), row_shapes, [rows_total, *flat]))
    outs = [(ways, part_size, cases, LANES)] * 2
    pieces = gather_panel(scatter_panel(*product(adjoint_kernel, first_sums, outs, [cols_total, rows_held])))
    sums = product(forward_kernel, pieces, row_shapes, [rows_total, cols_held])
    rows_out, share_out = (cases // n_case, row_groups * LANES), (share, width)
    sums, first_sums, pieces = lax.optimization_barrier((sums, first_sums, pieces))
    forward_one, adjoint_one = cut(cut_kernel, [*first_sums, *pieces], [rows_out, share_out])
    second_sums = over_case(sums)
    (by_share,) = product(last_kernel, second_sums, [(2, ways, share, width)], [cols_total, rows_held])
    summed = add_up(by_share[0], swap(by_share[1], "panel", 1))
    summed, second_sums = lax.optimization_barrier((summed, second_sums))
    adjoint_two = scatter_along(summed)
    (forward_two,) = cut(cut_last_kernel, second_sums, [rows_out])
    return (forward_one, adjoint_one, forward_two, adjoint_two)


def solution(mesh):
    in_specs = (
        P("panel", "case"),
        P(("panel", "case"), None, None),
        P(("panel", "case"), None),
        P(),
    )
    out_specs = (P("case", "panel"), P("panel", "case"), P("case", "panel"), P("panel", "case"))
    return jax.shard_map(shards, mesh=mesh, in_specs=in_specs, out_specs=out_specs, check_vma=False)
```

```python
import functools
import math

import jax
import jax.numpy as jnp
from jax import lax
from jax.experimental import pallas as pl
from jax.experimental.pallas import tpu as pltpu
from jax.sharding import PartitionSpec as P

B = 256
LANES = 128
PER = B // LANES
COPIES = 4
ROW_PARTS = 2
CHUNK = 768
VMEM_LIMIT = 12 * 1024 * 1024
FIRST_LIMIT = 50 * 1024 * 1024


def swap(value, axis, offset):
    count = lax.axis_size(axis)
    return lax.ppermute(value, axis, [(i, i ^ offset) for i in range(count)])


def add_up(*parts):
    total = parts[0].astype(jnp.float32)
    for part in parts[1:]:
        total = total + part.astype(jnp.float32)
    return total.astype(parts[0].dtype)


def spans(size, count):
    edges = [size * i // count for i in range(count + 1)]
    return [(a, b - a) for a, b in zip(edges, edges[1:])]


def start_hold(blocks_ref, held_ref, sems):
    copies = []
    for i, (start, size) in enumerate(spans(blocks_ref.shape[0], COPIES)):
        span = pl.ds(start, size)
        copies.append(pltpu.make_async_copy(blocks_ref.at[span], held_ref.at[span], sems.at[i]))
        copies[-1].start()
    return [(start, copy) for (start, _), copy in zip(spans(blocks_ref.shape[0], COPIES), copies)]


def pick_rows(values, index, size):
    values = values.astype(jnp.float32)
    picked = values[:size]
    for i in range(1, values.shape[0] // size):
        picked = jnp.where(index == i, values[i * size : (i + 1) * size], picked)
    return picked


def cut_rows(place_ref, parts, out_ref):
    at = 0
    for part in parts:
        for group in range(part.shape[0]):
            picked = pick_rows(part[group], place_ref[2], out_ref.shape[0])
            out_ref[:, at : at + LANES] = picked.astype(out_ref.dtype)
            at += LANES


def cut_kernel(ways, place_ref, *refs):
    parts, pieces, (rows_ref, share_ref) = refs[:ROW_PARTS], refs[ROW_PARTS:-2], refs[-2:]
    cut_rows(place_ref, parts, rows_ref)
    core, along = place_ref[0], place_ref[1]
    panel = along * 2 + core
    for side in range(2):
        for way in range(ways):
            piece = pieces[side * ways + way]
            at = ((core ^ side) * ways + (along ^ way)) * piece.shape[0]
            for group in range(piece.shape[0]):
                lanes = pl.ds(pl.multiple_of((at + group) * LANES, LANES), LANES)
                picked = pick_rows(piece[group], panel, share_ref.shape[0])
                share_ref[:, lanes] = picked.astype(share_ref.dtype)


def cut_last_kernel(ways, place_ref, *refs):
    cut_rows(place_ref, refs[:-1], refs[-1])


def add_products(entry_ref, gain_ref, load, block_refs, total, adjoint, copies=()):
    total[...] = jnp.zeros_like(total)
    at = 0
    for block_ref in block_refs:
        for slot in range(block_ref.shape[0]):
            for start, copy in copies:
                if start == slot:
                    copy.wait()
            row, col, level = entry_ref[at], entry_ref[at + 1], entry_ref[at + 2]
            at += 3
            scale = jnp.where(level >= 0, gain_ref[jnp.maximum(level, 0)], jnp.float32(0.0))
            source, target = (row, col) if adjoint else (col, row)
            term = lax.dot_general(
                load(source),
                block_ref[slot],
                (((1,), (0 if adjoint else 1,)), ((), ())),
                preferred_element_type=jnp.float32,
            )
            term = term * scale
            for piece in range(PER):
                total[target * PER + piece] += term[:, piece * LANES : (piece + 1) * LANES]


def load_from(x):
    def load(block):
        return jnp.concatenate([x[block * PER + piece] for piece in range(PER)], axis=1)

    return load


def write_parts(total, outs):
    at = 0
    for out_ref in outs:
        size = out_ref.shape[0]
        out_ref[...] = total[at : at + size].astype(out_ref.dtype)
        at += size


def join_parts(x, parts):
    at = 0
    for part in parts:
        size = part.shape[0]
        x[at : at + size] = part[...]
        at += size


def first_kernel(ways, entry_ref, gain_ref, place_ref, *refs):
    count = 2 * ways
    pieces, blocks_ref, outs = refs[:count], refs[count], refs[count + 1 : -5]
    total, wide, x, held_ref, sems = refs[-5:]
    copies = start_hold(blocks_ref, held_ref, sems)
    core, along = place_ref[0], place_ref[1]
    share, width = pieces[0].shape
    chunk = math.gcd(width, CHUNK)

    def assemble(step, carry):
        lanes = pl.ds(pl.multiple_of(step * chunk, chunk), chunk)
        rows = [piece[:, lanes].astype(jnp.float32) for piece in pieces]
        bit, place = 1, along + core * ways
        while bit < count:
            flip = (place & bit) != 0
            rows = [jnp.where(flip, rows[i ^ bit], rows[i]) for i in range(count)]
            bit *= 2
        for side in range(2):
            for way in range(ways):
                at = (2 * way + side) * share
                wide[at : at + share, lanes] = rows[side * ways + way]
        x[:, lanes] = wide[:, lanes].astype(x.dtype)
        return carry

    lax.fori_loop(0, width // chunk, assemble, 0)

    def load(block):
        return x[:, pl.ds(pl.multiple_of(block * B, B), B)]

    add_products(entry_ref, gain_ref, load, [held_ref], total, False, copies)
    write_parts(total, outs)


def forward_kernel(ways, entry_ref, gain_ref, place_ref, *refs):
    count = 2 * ways
    pieces, block_refs, outs = refs[:count], refs[count : count + 1], refs[count + 1 : -2]
    total, x = refs[-2:]
    core, along = place_ref[0], place_ref[1]
    size = pieces[0].shape[0]
    for side in range(2):
        for way in range(ways):
            at = ((core ^ side) * ways + (along ^ way)) * size
            x[pl.ds(at, size)] = pieces[side * ways + way][...]
    add_products(entry_ref, gain_ref, load_from(x), block_refs, total, False)
    write_parts(total, outs)


def adjoint_kernel(ways, entry_ref, gain_ref, place_ref, *refs):
    parts, block_refs = refs[:ROW_PARTS], refs[ROW_PARTS : ROW_PARTS + 1]
    outs = refs[ROW_PARTS + 1 : -2]
    total, x = refs[-2:]
    join_parts(x, parts)
    add_products(entry_ref, gain_ref, load_from(x), block_refs, total, True)
    core, along = place_ref[0], place_ref[1]
    size = outs[0].shape[1]
    for side, out_ref in enumerate(outs):
        for way in range(ways):
            at = ((core ^ side) * ways + (along ^ way)) * size
            out_ref[way] = total[pl.ds(at, size)].astype(out_ref.dtype)


def last_kernel(ways, entry_ref, gain_ref, place_ref, *refs):
    parts, block_refs = refs[:ROW_PARTS], refs[ROW_PARTS : ROW_PARTS + 1]
    out_ref, total, x = refs[ROW_PARTS + 1 :]
    join_parts(x, parts)
    add_products(entry_ref, gain_ref, load_from(x), block_refs, total, True)
    core, along = place_ref[0], place_ref[1]
    share = out_ref.shape[2]
    for group in range(total.shape[0]):
        values = total[group].astype(out_ref.dtype)
        for index in range(2 * ways):
            piece = values[index * share : (index + 1) * share]
            out_ref[core ^ (index % 2), along ^ (index // 2), :, group * LANES : (group + 1) * LANES] = piece


def shards(strengths, blocks, pattern, level_gain):
    n_panel = lax.axis_size("panel")
    n_case = lax.axis_size("case")
    ways = n_panel // 2
    share, width = strengths.shape
    cases = share * n_panel
    slots = blocks.shape[0]
    col_blocks = width // B
    row_blocks = col_blocks * n_case // n_panel
    col_groups = col_blocks * PER
    row_groups = row_blocks * PER
    panel = lax.axis_index("panel")
    case = lax.axis_index("case")
    core = panel % 2
    along = panel // 2
    value = strengths.dtype
    row_cuts = spans(row_groups, ROW_PARTS)
    part_size = col_groups // n_panel

    place = jnp.stack([core, along, case]).astype(jnp.int32)
    first = jnp.stack([panel * row_blocks, case * col_blocks, 0]).astype(jnp.int32)
    entry = jnp.where(pattern[:, 2:3] < 0, jnp.array([0, 0, -1], jnp.int32), pattern - first).reshape(-1)

    smem = pl.BlockSpec(memory_space=pltpu.SMEM)
    vmem = pl.BlockSpec(memory_space=pltpu.VMEM)

    params = pltpu.CompilerParams(vmem_limit_bytes=VMEM_LIMIT)
    def cut(kernel, vectors, outs):
        return pl.pallas_call(
            functools.partial(kernel, ways),
            out_shape=[jax.ShapeDtypeStruct(shape, value) for shape in outs],
            in_specs=[smem] + [vmem] * len(vectors),
            out_specs=[vmem] * len(outs),
            compiler_params=params,
            cost_estimate=pl.CostEstimate(flops=0, bytes_accessed=8 * share * width, transcendentals=0),
        )(place, *vectors)

    def product(kernel, vectors, outs, scratch, limit=VMEM_LIMIT, space=pltpu.VMEM):
        small = (entry, level_gain, place)
        return pl.pallas_call(
            functools.partial(kernel, ways),
            out_shape=[jax.ShapeDtypeStruct(shape, value) for shape in outs],
            in_specs=[smem] * len(small) + [vmem] * len(vectors) + [pl.BlockSpec(memory_space=space)],
            out_specs=[vmem] * len(outs),
            scratch_shapes=scratch,
            compiler_params=pltpu.CompilerParams(vmem_limit_bytes=limit),
            cost_estimate=pl.CostEstimate(
                flops=2 * cases * slots * B * B, bytes_accessed=2 * slots * B * B, transcendentals=0
            ),
        )(*small, *vectors, blocks)

    def scratch(groups, kind):
        return pltpu.VMEM((groups, cases, LANES), kind)

    rows_total, rows_held = scratch(row_groups, jnp.float32), scratch(row_groups, value)
    cols_total, cols_held = scratch(col_groups, jnp.float32), scratch(col_groups, value)
    flat = [pltpu.VMEM((cases, width), kind) for kind in (jnp.float32, value)]
    row_shapes = [(size, cases, LANES) for _, size in row_cuts]

    def over_case(parts):
        bits = [1 << b for b in range(n_case.bit_length() - 1)]
        parts = list(parts)
        for step in range(len(bits)):
            arrived = [swap(part, "case", bits[(step + i) % len(bits)]) for i, part in enumerate(parts)]
            parts = [add_up(part, one) for part, one in zip(parts, arrived)]
        return parts

    def scatter_panel(mine, theirs):
        return scatter_along(add_up(mine, swap(theirs, "panel", 1)))

    far_first = sorted(range(1, ways), key=lambda way: way & (ways // 2) == 0)

    def along_swaps(part_of):
        arrived = {way: swap(part_of(way), "panel", 2 * way) for way in far_first}
        return [arrived[way] for way in range(1, ways)]

    def scatter_along(summed):
        return add_up(summed[0], *along_swaps(lambda way: summed[way]))

    def gather_panel(part):
        same = [part, *along_swaps(lambda way: part)]
        return same + [swap(one, "panel", 1) for one in same]

    own_copy = [pltpu.VMEM(blocks.shape, blocks.dtype), pltpu.SemaphoreType.DMA((COPIES,))]
    scratches = [rows_total, *flat, *own_copy]
    first_sums = over_case(
        product(first_kernel, gather_panel(strengths), row_shapes, scratches, FIRST_LIMIT, pl.ANY)
    )
    outs = [(ways, part_size, cases, LANES)] * 2
    pieces = gather_panel(scatter_panel(*product(adjoint_kernel, first_sums, outs, [cols_total, rows_held])))
    sums = product(forward_kernel, pieces, row_shapes, [rows_total, cols_held])
    rows_out, share_out = (cases // n_case, row_groups * LANES), (share, width)
    sums, first_sums, pieces = lax.optimization_barrier((sums, first_sums, pieces))
    forward_one, adjoint_one = cut(cut_kernel, [*first_sums, *pieces], [rows_out, share_out])
    second_sums = over_case(sums)
    (by_share,) = product(last_kernel, second_sums, [(2, ways, share, width)], [cols_total, rows_held])
    summed = add_up(by_share[0], swap(by_share[1], "panel", 1))
    summed, second_sums = lax.optimization_barrier((summed, second_sums))
    adjoint_two = scatter_along(summed)
    (forward_two,) = cut(cut_last_kernel, second_sums, [rows_out])
    return (forward_one, adjoint_one, forward_two, adjoint_two)


def solution(mesh):
    in_specs = (
        P("panel", "case"),
        P(("panel", "case"), None, None),
        P(("panel", "case"), None),
        P(),
    )
    out_specs = (P("case", "panel"), P("panel", "case"), P("case", "panel"), P("panel", "case"))
    return jax.shard_map(shards, mesh=mesh, in_specs=in_specs, out_specs=out_specs, check_vma=False)
```

```python
import functools
import math

import jax
import jax.numpy as jnp
from jax import lax
from jax.experimental import pallas as pl
from jax.experimental.pallas import tpu as pltpu
from jax.sharding import PartitionSpec as P

B = 256
LANES = 128
PER = B // LANES
COPIES = 8
ROW_PARTS = 2
CHUNK = 512
UNROLL = 16
VMEM_LIMIT = 12 * 1024 * 1024
FIRST_LIMIT = 50 * 1024 * 1024


def swap(value, axis, offset):
    count = lax.axis_size(axis)
    return lax.ppermute(value, axis, [(i, i ^ offset) for i in range(count)])


def add_up(*parts):
    total = parts[0].astype(jnp.float32)
    for part in parts[1:]:
        total = total + part.astype(jnp.float32)
    return total.astype(parts[0].dtype)


def spans(size, count):
    edges = [size * i // count for i in range(count + 1)]
    return [(a, b - a) for a, b in zip(edges, edges[1:])]


def start_hold(blocks_ref, held_ref, sems):
    copies = []
    for i, (start, size) in enumerate(spans(blocks_ref.shape[0], COPIES)):
        span = pl.ds(start, size)
        copies.append(pltpu.make_async_copy(blocks_ref.at[span], held_ref.at[span], sems.at[i]))
        copies[-1].start()
    return [(start, copy) for (start, _), copy in zip(spans(blocks_ref.shape[0], COPIES), copies)]


def pick_rows(values, index, size):
    values = values.astype(jnp.float32)
    picked = values[:size]
    for i in range(1, values.shape[0] // size):
        picked = jnp.where(index == i, values[i * size : (i + 1) * size], picked)
    return picked


def cut_rows(place_ref, parts, out_ref):
    at = 0
    for part in parts:
        for group in range(part.shape[0]):
            picked = pick_rows(part[group], place_ref[2], out_ref.shape[0])
            out_ref[:, at : at + LANES] = picked.astype(out_ref.dtype)
            at += LANES


def cut_kernel(ways, place_ref, *refs):
    parts, pieces, (rows_ref, share_ref) = refs[:ROW_PARTS], refs[ROW_PARTS:-2], refs[-2:]
    cut_rows(place_ref, parts, rows_ref)
    core, along = place_ref[0], place_ref[1]
    panel = along * 2 + core
    for side in range(2):
        for way in range(ways):
            piece = pieces[side * ways + way]
            at = ((core ^ side) * ways + (along ^ way)) * piece.shape[0]
            for group in range(piece.shape[0]):
                lanes = pl.ds(pl.multiple_of((at + group) * LANES, LANES), LANES)
                picked = pick_rows(piece[group], panel, share_ref.shape[0])
                share_ref[:, lanes] = picked.astype(share_ref.dtype)


def cut_last_kernel(ways, place_ref, *refs):
    cut_rows(place_ref, refs[:-1], refs[-1])


def add_products(entry_ref, scale_ref, load, block_refs, total, adjoint, copies=()):
    total[...] = jnp.zeros_like(total)
    at = 0
    for block_ref in block_refs:
        for slot in range(block_ref.shape[0]):
            for start, copy in copies:
                if start == slot:
                    copy.wait()
            row, col, scale = entry_ref[2 * at], entry_ref[2 * at + 1], scale_ref[at]
            at += 1
            source, target = (row, col) if adjoint else (col, row)
            term = lax.dot_general(
                load(source),
                block_ref[slot],
                (((1,), (0 if adjoint else 1,)), ((), ())),
                preferred_element_type=jnp.float32,
            )
            term = term * scale
            for piece in range(PER):
                total[target * PER + piece] += term[:, piece * LANES : (piece + 1) * LANES]


def load_from(x):
    def load(block):
        return jnp.concatenate([x[block * PER + piece] for piece in range(PER)], axis=1)

    return load


def write_parts(total, outs):
    at = 0
    for out_ref in outs:
        size = out_ref.shape[0]
        out_ref[...] = total[at : at + size].astype(out_ref.dtype)
        at += size


def join_parts(x, parts):
    at = 0
    for part in parts:
        size = part.shape[0]
        x[at : at + size] = part[...]
        at += size


def first_kernel(ways, entry_ref, scale_ref, place_ref, *refs):
    count = 2 * ways
    pieces, blocks_ref, outs = refs[:count], refs[count], refs[count + 1 : -5]
    total, wide, x, held_ref, sems = refs[-5:]
    copies = start_hold(blocks_ref, held_ref, sems)
    core, along = place_ref[0], place_ref[1]
    share, width = pieces[0].shape
    chunk = math.gcd(width, CHUNK)

    def assemble(step, carry):
        lanes = pl.ds(pl.multiple_of(step * chunk, chunk), chunk)
        rows = [piece[:, lanes].astype(jnp.float32) for piece in pieces]
        bit, place = 1, along + core * ways
        while bit < count:
            flip = (place & bit) != 0
            rows = [jnp.where(flip, rows[i ^ bit], rows[i]) for i in range(count)]
            bit *= 2
        for side in range(2):
            for way in range(ways):
                at = (2 * way + side) * share
                wide[at : at + share, lanes] = rows[side * ways + way]
        x[:, lanes] = wide[:, lanes].astype(x.dtype)
        return carry

    lax.fori_loop(0, width // chunk, assemble, 0)

    def load(block):
        return x[:, pl.ds(pl.multiple_of(block * B, B), B)]

    add_products(entry_ref, scale_ref, load, [held_ref], total, False, copies)
    write_parts(total, outs)


def forward_kernel(ways, entry_ref, scale_ref, place_ref, *refs):
    count = 2 * ways
    pieces, block_refs, outs = refs[:count], refs[count : count + 1], refs[count + 1 : -2]
    total, x = refs[-2:]
    core, along = place_ref[0], place_ref[1]
    size = pieces[0].shape[0]
    for side in range(2):
        for way in range(ways):
            at = ((core ^ side) * ways + (along ^ way)) * size
            x[pl.ds(at, size)] = pieces[side * ways + way][...]
    add_products(entry_ref, scale_ref, load_from(x), block_refs, total, False)
    write_parts(total, outs)


def adjoint_kernel(ways, entry_ref, scale_ref, place_ref, *refs):
    parts, block_refs = refs[:ROW_PARTS], refs[ROW_PARTS : ROW_PARTS + 1]
    outs = refs[ROW_PARTS + 1 : -2]
    total, x = refs[-2:]
    join_parts(x, parts)
    add_products(entry_ref, scale_ref, load_from(x), block_refs, total, True)
    core, along = place_ref[0], place_ref[1]
    size = outs[0].shape[1]
    for side, out_ref in enumerate(outs):
        for way in range(ways):
            at = ((core ^ side) * ways + (along ^ way)) * size
            out_ref[way] = total[pl.ds(at, size)].astype(out_ref.dtype)


def last_kernel(ways, entry_ref, scale_ref, place_ref, *refs):
    parts, block_refs = refs[:ROW_PARTS], refs[ROW_PARTS : ROW_PARTS + 1]
    out_ref, total, x = refs[ROW_PARTS + 1 :]
    join_parts(x, parts)
    add_products(entry_ref, scale_ref, load_from(x), block_refs, total, True)
    core, along = place_ref[0], place_ref[1]
    share = out_ref.shape[2]
    groups = math.gcd(total.shape[0], UNROLL)

    def write(step, carry):
        for i in range(groups):
            group = step * groups + i
            lanes = pl.ds(pl.multiple_of(group * LANES, LANES), LANES)
            values = total[group].astype(out_ref.dtype)
            for index in range(2 * ways):
                piece = values[index * share : (index + 1) * share]
                out_ref[core ^ (index % 2), along ^ (index // 2), :, lanes] = piece
        return carry

    lax.fori_loop(0, total.shape[0] // groups, write, 0)


def shards(strengths, blocks, pattern, level_gain):
    n_panel = lax.axis_size("panel")
    n_case = lax.axis_size("case")
    ways = n_panel // 2
    share, width = strengths.shape
    cases = share * n_panel
    slots = blocks.shape[0]
    col_blocks = width // B
    row_blocks = col_blocks * n_case // n_panel
    col_groups = col_blocks * PER
    row_groups = row_blocks * PER
    panel = lax.axis_index("panel")
    case = lax.axis_index("case")
    core = panel % 2
    along = panel // 2
    value = strengths.dtype
    row_cuts = spans(row_groups, ROW_PARTS)
    part_size = col_groups // n_panel

    place = jnp.stack([core, along, case]).astype(jnp.int32)
    first = jnp.stack([panel * row_blocks, case * col_blocks]).astype(jnp.int32)
    entry = jnp.where(pattern[:, 2:] >= 0, pattern[:, :2] - first, 0).reshape(-1)
    level_ids = jnp.arange(level_gain.shape[0], dtype=jnp.int32)
    scale = jnp.sum(jnp.where(pattern[:, 2:] == level_ids, level_gain, jnp.float32(0.0)), axis=1)

    smem = pl.BlockSpec(memory_space=pltpu.SMEM)
    vmem = pl.BlockSpec(memory_space=pltpu.VMEM)

    params = pltpu.CompilerParams(vmem_limit_bytes=VMEM_LIMIT)
    def cut(kernel, vectors, outs):
        return pl.pallas_call(
            functools.partial(kernel, ways),
            out_shape=[jax.ShapeDtypeStruct(shape, value) for shape in outs],
            in_specs=[smem] + [vmem] * len(vectors),
            out_specs=[vmem] * len(outs),
            compiler_params=params,
            cost_estimate=pl.CostEstimate(flops=0, bytes_accessed=8 * share * width, transcendentals=0),
        )(place, *vectors)

    def product(kernel, vectors, outs, scratch, limit=VMEM_LIMIT, space=None):
        small = (entry, scale, place)
        return pl.pallas_call(
            functools.partial(kernel, ways),
            out_shape=[jax.ShapeDtypeStruct(shape, value) for shape in outs],
            in_specs=[smem] * len(small) + [vmem] * len(vectors) + [space or vmem],
            out_specs=[vmem] * len(outs),
            scratch_shapes=scratch,
            compiler_params=pltpu.CompilerParams(vmem_limit_bytes=limit),
            cost_estimate=pl.CostEstimate(
                flops=2 * cases * slots * B * B, bytes_accessed=2 * slots * B * B, transcendentals=0
            ),
        )(*small, *vectors, blocks)

    def scratch(groups, kind):
        return pltpu.VMEM((groups, cases, LANES), kind)

    rows_total, rows_held = scratch(row_groups, jnp.float32), scratch(row_groups, value)
    cols_total, cols_held = scratch(col_groups, jnp.float32), scratch(col_groups, value)
    flat = [pltpu.VMEM((cases, width), kind) for kind in (jnp.float32, value)]
    row_shapes = [(size, cases, LANES) for _, size in row_cuts]

    def over_case(parts):
        bits = [1 << b for b in range(n_case.bit_length() - 1)]
        parts = list(parts)
        for step in range(len(bits)):
            arrived = [swap(part, "case", bits[(step + i) % len(bits)]) for i, part in enumerate(parts)]
            parts = [add_up(part, one) for part, one in zip(parts, arrived)]
        return parts

    def scatter_panel(mine, theirs):
        return scatter_along(add_up(mine, swap(theirs, "panel", 1)))

    far_first = sorted(range(1, ways), key=lambda way: way & (ways // 2) == 0)

    def along_swaps(part_of):
        arrived = {way: swap(part_of(way), "panel", 2 * way) for way in far_first}
        return [arrived[way] for way in range(1, ways)]

    def scatter_along(summed):
        return add_up(summed[0], *along_swaps(lambda way: summed[way]))

    def gather_panel(part):
        same = [part, *along_swaps(lambda way: part)]
        return same + [swap(one, "panel", 1) for one in same]

    mine = jnp.where(core >= 0, strengths, 0)
    own_copy = [pltpu.VMEM(blocks.shape, blocks.dtype), pltpu.SemaphoreType.DMA((COPIES,))]
    scratches = [rows_total, *flat, *own_copy]
    first_sums = over_case(
        product(first_kernel, [mine, *gather_panel(strengths)[1:]], row_shapes, scratches, FIRST_LIMIT, pl.BlockSpec(memory_space=pl.ANY))
    )
    outs = [(ways, part_size, cases, LANES)] * 2
    pieces = gather_panel(scatter_panel(*product(adjoint_kernel, first_sums, outs, [cols_total, rows_held])))
    sums = product(forward_kernel, pieces, row_shapes, [rows_total, cols_held])
    rows_out, share_out = (cases // n_case, row_groups * LANES), (share, width)
    sums, first_sums, pieces = lax.optimization_barrier((sums, first_sums, pieces))
    forward_one, adjoint_one = cut(cut_kernel, [*first_sums, *pieces], [rows_out, share_out])
    second_sums = over_case(sums)
    (by_share,) = product(last_kernel, second_sums, [(2, ways, share, width)], [cols_total, rows_held])
    summed = add_up(by_share[0], swap(by_share[1], "panel", 1))
    summed, second_sums = lax.optimization_barrier((summed, second_sums))
    adjoint_two = scatter_along(summed)
    (forward_two,) = cut(cut_last_kernel, second_sums, [rows_out])
    return (forward_one, adjoint_one, forward_two, adjoint_two)


def solution(mesh):
    in_specs = (
        P("panel", "case"),
        P(("panel", "case"), None, None),
        P(("panel", "case"), None),
        P(),
    )
    out_specs = (P("case", "panel"), P("panel", "case"), P("case", "panel"), P("panel", "case"))
    return jax.shard_map(shards, mesh=mesh, in_specs=in_specs, out_specs=out_specs, check_vma=False)
```

```python
import functools
import math

import jax
import jax.numpy as jnp
from jax import lax
from jax.experimental import pallas as pl
from jax.experimental.pallas import tpu as pltpu
from jax.sharding import PartitionSpec as P

B = 256
LANES = 128
PER = B // LANES
COPIES = 4
ROW_PARTS = 2
CHUNK = 1024
UNROLL = 48
VMEM_LIMIT = 12 * 1024 * 1024
FIRST_LIMIT = 50 * 1024 * 1024


def swap(value, axis, offset):
    count = lax.axis_size(axis)
    return lax.ppermute(value, axis, [(i, i ^ offset) for i in range(count)])


def add_up(*parts):
    total = parts[0].astype(jnp.float32)
    for part in parts[1:]:
        total = total + part.astype(jnp.float32)
    return total.astype(parts[0].dtype)


def spans(size, count):
    edges = [size * i // count for i in range(count + 1)]
    return [(a, b - a) for a, b in zip(edges, edges[1:])]


def start_hold(blocks_ref, held_ref, sems):
    size = held_ref.shape[0]
    before = blocks_ref.shape[0] - size
    copies = []
    for i, (start, count) in enumerate(spans(size, COPIES)):
        source = blocks_ref.at[pl.ds(before + start, count)]
        copy = pltpu.make_async_copy(source, held_ref.at[pl.ds(start, count)], sems.at[i])
        copy.start()
        copies.append((before + start, copy))
    return copies


def pick_rows(values, index, size):
    values = values.astype(jnp.float32)
    picked = values[:size]
    for i in range(1, values.shape[0] // size):
        picked = jnp.where(index == i, values[i * size : (i + 1) * size], picked)
    return picked


def cut_rows(place_ref, parts, out_ref):
    at = 0
    for part in parts:
        for group in range(part.shape[0]):
            picked = pick_rows(part[group], place_ref[2], out_ref.shape[0])
            out_ref[:, at : at + LANES] = picked.astype(out_ref.dtype)
            at += LANES


def cut_kernel(ways, place_ref, *refs):
    parts, pieces, (rows_ref, share_ref) = refs[:ROW_PARTS], refs[ROW_PARTS:-2], refs[-2:]
    cut_rows(place_ref, parts, rows_ref)
    core, along = place_ref[0], place_ref[1]
    panel = along * 2 + core
    for side in range(2):
        for way in range(ways):
            piece = pieces[side * ways + way]
            at = ((core ^ side) * ways + (along ^ way)) * piece.shape[0]
            for group in range(piece.shape[0]):
                lanes = pl.ds(pl.multiple_of((at + group) * LANES, LANES), LANES)
                picked = pick_rows(piece[group], panel, share_ref.shape[0])
                share_ref[:, lanes] = picked.astype(share_ref.dtype)


def cut_last_kernel(ways, place_ref, *refs):
    cut_rows(place_ref, refs[:-1], refs[-1])


def add_products(entry_ref, scale_ref, load, block_refs, total, adjoint, copies=()):
    total[...] = jnp.zeros_like(total)
    at = 0
    for block_ref in block_refs:
        for slot in range(block_ref.shape[0]):
            for start, copy in copies:
                if start == at:
                    copy.wait()
            row, col, scale = entry_ref[2 * at], entry_ref[2 * at + 1], scale_ref[at]
            at += 1
            source, target = (row, col) if adjoint else (col, row)
            term = lax.dot_general(
                load(source),
                block_ref[slot],
                (((1,), (0 if adjoint else 1,)), ((), ())),
                preferred_element_type=jnp.float32,
            )
            term = term * scale
            for piece in range(PER):
                total[target * PER + piece] += term[:, piece * LANES : (piece + 1) * LANES]


def load_from(x):
    def load(block):
        return jnp.concatenate([x[block * PER + piece] for piece in range(PER)], axis=1)

    return load


def write_parts(total, outs):
    at = 0
    for out_ref in outs:
        size = out_ref.shape[0]
        out_ref[...] = total[at : at + size].astype(out_ref.dtype)
        at += size


def join_parts(x, parts):
    at = 0
    for part in parts:
        size = part.shape[0]
        x[at : at + size] = part[...]
        at += size


def first_kernel(ways, entry_ref, scale_ref, place_ref, *refs):
    count = 2 * ways
    pieces, ready_ref, blocks_ref, outs = refs[:count], refs[count], refs[count + 1], refs[count + 2 : -5]
    total, wide, x, held_ref, sems = refs[-5:]
    copies = start_hold(blocks_ref, held_ref, sems)
    core, along = place_ref[0], place_ref[1]
    share, width = pieces[0].shape
    chunk = math.gcd(width, CHUNK)

    def assemble(step, carry):
        lanes = pl.ds(pl.multiple_of(step * chunk, chunk), chunk)
        rows = [piece[:, lanes].astype(jnp.float32) for piece in pieces]
        bit, place = 1, along + core * ways
        while bit < count:
            flip = (place & bit) != 0
            rows = [jnp.where(flip, rows[i ^ bit], rows[i]) for i in range(count)]
            bit *= 2
        for side in range(2):
            for way in range(ways):
                at = (2 * way + side) * share
                wide[at : at + share, lanes] = rows[side * ways + way]
        x[:, lanes] = wide[:, lanes].astype(x.dtype)
        return carry

    lax.fori_loop(0, width // chunk, assemble, 0)

    def load(block):
        return x[:, pl.ds(pl.multiple_of(block * B, B), B)]

    add_products(entry_ref, scale_ref, load, [ready_ref, held_ref], total, False, copies)
    write_parts(total, outs)


def forward_kernel(ways, entry_ref, scale_ref, place_ref, *refs):
    count = 2 * ways
    pieces, block_refs, outs = refs[:count], refs[count : count + 1], refs[count + 1 : -2]
    total, x = refs[-2:]
    core, along = place_ref[0], place_ref[1]
    size = pieces[0].shape[0]
    for side in range(2):
        for way in range(ways):
            at = ((core ^ side) * ways + (along ^ way)) * size
            x[pl.ds(at, size)] = pieces[side * ways + way][...]
    add_products(entry_ref, scale_ref, load_from(x), block_refs, total, False)
    write_parts(total, outs)


def adjoint_kernel(ways, entry_ref, scale_ref, place_ref, *refs):
    parts, block_refs = refs[:ROW_PARTS], refs[ROW_PARTS : ROW_PARTS + 1]
    outs = refs[ROW_PARTS + 1 : -2]
    total, x = refs[-2:]
    join_parts(x, parts)
    add_products(entry_ref, scale_ref, load_from(x), block_refs, total, True)
    core, along = place_ref[0], place_ref[1]
    size = outs[0].shape[1]
    for side, out_ref in enumerate(outs):
        for way in range(ways):
            at = ((core ^ side) * ways + (along ^ way)) * size
            out_ref[way] = total[pl.ds(at, size)].astype(out_ref.dtype)


def last_kernel(ways, entry_ref, scale_ref, place_ref, *refs):
    parts, block_refs = refs[:ROW_PARTS], refs[ROW_PARTS : ROW_PARTS + 1]
    out_ref, total, x = refs[ROW_PARTS + 1 :]
    join_parts(x, parts)
    add_products(entry_ref, scale_ref, load_from(x), block_refs, total, True)
    core, along = place_ref[0], place_ref[1]
    share = out_ref.shape[2]
    groups = math.gcd(total.shape[0], UNROLL)

    def write(step, carry):
        for i in range(groups):
            group = step * groups + i
            lanes = pl.ds(pl.multiple_of(group * LANES, LANES), LANES)
            values = total[group].astype(out_ref.dtype)
            for index in range(2 * ways):
                piece = values[index * share : (index + 1) * share]
                out_ref[core ^ (index % 2), along ^ (index // 2), :, lanes] = piece
        return carry

    lax.fori_loop(0, total.shape[0] // groups, write, 0)


def shards(strengths, blocks, pattern, level_gain):
    n_panel = lax.axis_size("panel")
    n_case = lax.axis_size("case")
    ways = n_panel // 2
    share, width = strengths.shape
    cases = share * n_panel
    slots = blocks.shape[0]
    col_blocks = width // B
    row_blocks = col_blocks * n_case // n_panel
    col_groups = col_blocks * PER
    row_groups = row_blocks * PER
    panel = lax.axis_index("panel")
    case = lax.axis_index("case")
    core = panel % 2
    along = panel // 2
    value = strengths.dtype
    row_cuts = spans(row_groups, ROW_PARTS)
    part_size = col_groups // n_panel

    place = jnp.stack([core, along, case]).astype(jnp.int32)
    first = jnp.stack([panel * row_blocks, case * col_blocks]).astype(jnp.int32)
    entry = jnp.where(pattern[:, 2:] >= 0, pattern[:, :2] - first, 0).reshape(-1)
    level_ids = jnp.arange(level_gain.shape[0], dtype=jnp.int32)
    scale = jnp.sum(jnp.where(pattern[:, 2:] == level_ids, level_gain, jnp.float32(0.0)), axis=1)

    smem = pl.BlockSpec(memory_space=pltpu.SMEM)
    vmem = pl.BlockSpec(memory_space=pltpu.VMEM)

    params = pltpu.CompilerParams(vmem_limit_bytes=VMEM_LIMIT)
    def cut(kernel, vectors, outs):
        return pl.pallas_call(
            functools.partial(kernel, ways),
            out_shape=[jax.ShapeDtypeStruct(shape, value) for shape in outs],
            in_specs=[smem] + [vmem] * len(vectors),
            out_specs=[vmem] * len(outs),
            compiler_params=params,
            cost_estimate=pl.CostEstimate(flops=0, bytes_accessed=8 * share * width, transcendentals=0),
        )(place, *vectors)

    def product(kernel, vectors, outs, scratch, limit=VMEM_LIMIT, space=None):
        small = (entry, scale, place)
        return pl.pallas_call(
            functools.partial(kernel, ways),
            out_shape=[jax.ShapeDtypeStruct(shape, value) for shape in outs],
            in_specs=[smem] * len(small) + [vmem] * len(vectors) + [space or vmem],
            out_specs=[vmem] * len(outs),
            scratch_shapes=scratch,
            compiler_params=pltpu.CompilerParams(vmem_limit_bytes=limit),
            cost_estimate=pl.CostEstimate(
                flops=2 * cases * slots * B * B, bytes_accessed=2 * slots * B * B, transcendentals=0
            ),
        )(*small, *vectors, blocks)

    def scratch(groups, kind):
        return pltpu.VMEM((groups, cases, LANES), kind)

    rows_total, rows_held = scratch(row_groups, jnp.float32), scratch(row_groups, value)
    cols_total, cols_held = scratch(col_groups, jnp.float32), scratch(col_groups, value)
    flat = [pltpu.VMEM((cases, width), kind) for kind in (jnp.float32, value)]
    row_shapes = [(size, cases, LANES) for _, size in row_cuts]

    def over_case(parts):
        bits = [1 << b for b in range(n_case.bit_length() - 1)]
        parts = list(parts)
        for step in range(len(bits)):
            arrived = [swap(part, "case", bits[(step + i) % len(bits)]) for i, part in enumerate(parts)]
            parts = [add_up(part, one) for part, one in zip(parts, arrived)]
        return parts

    def scatter_panel(mine, theirs):
        return scatter_along(add_up(mine, swap(theirs, "panel", 1)))

    far_first = sorted(range(1, ways), key=lambda way: way & (ways // 2) == 0)

    def along_swaps(part_of):
        arrived = {way: swap(part_of(way), "panel", 2 * way) for way in far_first}
        return [arrived[way] for way in range(1, ways)]

    def scatter_along(summed):
        return add_up(summed[0], *along_swaps(lambda way: summed[way]))

    def gather_panel(part):
        same = [part, *along_swaps(lambda way: part)]
        return same + [swap(one, "panel", 1) for one in same]

    mine = jnp.where(core >= 0, strengths, 0)
    ready = jnp.where(core >= 0, blocks[: slots // 2], 0)
    own_copy = [pltpu.VMEM((slots - slots // 2, B, B), blocks.dtype), pltpu.SemaphoreType.DMA((COPIES,))]
    scratches = [rows_total, *flat, *own_copy]
    first_sums = over_case(
        product(first_kernel, [mine, *gather_panel(strengths)[1:], ready], row_shapes, scratches, FIRST_LIMIT, pl.BlockSpec(memory_space=pl.ANY))
    )
    outs = [(ways, part_size, cases, LANES)] * 2
    pieces = gather_panel(scatter_panel(*product(adjoint_kernel, first_sums, outs, [cols_total, rows_held])))
    sums = product(forward_kernel, pieces, row_shapes, [rows_total, cols_held])
    rows_out, share_out = (cases // n_case, row_groups * LANES), (share, width)
    sums, first_sums, pieces = lax.optimization_barrier((sums, first_sums, pieces))
    forward_one, adjoint_one = cut(cut_kernel, [*first_sums, *pieces], [rows_out, share_out])
    second_sums = over_case(sums)
    (by_share,) = product(last_kernel, second_sums, [(2, ways, share, width)], [cols_total, rows_held])
    summed = add_up(by_share[0], swap(by_share[1], "panel", 1))
    summed, second_sums = lax.optimization_barrier((summed, second_sums))
    adjoint_two = scatter_along(summed)
    (forward_two,) = cut(cut_last_kernel, second_sums, [rows_out])
    return (forward_one, adjoint_one, forward_two, adjoint_two)


def solution(mesh):
    in_specs = (
        P("panel", "case"),
        P(("panel", "case"), None, None),
        P(("panel", "case"), None),
        P(),
    )
    out_specs = (P("case", "panel"), P("panel", "case"), P("case", "panel"), P("panel", "case"))
    return jax.shard_map(shards, mesh=mesh, in_specs=in_specs, out_specs=out_specs, check_vma=False)
```

```python
import functools
import math

import jax
import jax.numpy as jnp
from jax import lax
from jax.experimental import pallas as pl
from jax.experimental.pallas import tpu as pltpu
from jax.sharding import PartitionSpec as P

B = 256
LANES = 128
PER = B // LANES
COPIES = 4
ROW_PARTS = 1
CHUNK = 1024
UNROLL = 96
VMEM_LIMIT = 12 * 1024 * 1024
FIRST_LIMIT = 50 * 1024 * 1024


def swap(value, axis, offset):
    count = lax.axis_size(axis)
    return lax.ppermute(value, axis, [(i, i ^ offset) for i in range(count)])


def add_up(*parts):
    total = parts[0].astype(jnp.float32)
    for part in parts[1:]:
        total = total + part.astype(jnp.float32)
    return total.astype(parts[0].dtype)


def spans(size, count):
    edges = [size * i // count for i in range(count + 1)]
    return [(a, b - a) for a, b in zip(edges, edges[1:])]


def start_hold(blocks_ref, held_ref, sems):
    size = held_ref.shape[0]
    before = blocks_ref.shape[0] - size
    copies = []
    for i, (start, count) in enumerate(spans(size, COPIES)):
        source = blocks_ref.at[pl.ds(before + start, count)]
        copy = pltpu.make_async_copy(source, held_ref.at[pl.ds(start, count)], sems.at[i])
        copy.start()
        copies.append((before + start, copy))
    return copies


def pick_rows(values, index, size):
    values = values.astype(jnp.float32)
    picked = values[:size]
    for i in range(1, values.shape[0] // size):
        picked = jnp.where(index == i, values[i * size : (i + 1) * size], picked)
    return picked


def cut_rows(place_ref, parts, out_ref):
    at = 0
    for part in parts:
        for group in range(part.shape[0]):
            picked = pick_rows(part[group], place_ref[2], out_ref.shape[0])
            out_ref[:, at : at + LANES] = picked.astype(out_ref.dtype)
            at += LANES


def cut_kernel(ways, place_ref, *refs):
    parts, pieces, (rows_ref, share_ref) = refs[:ROW_PARTS], refs[ROW_PARTS:-2], refs[-2:]
    cut_rows(place_ref, parts, rows_ref)
    core, along = place_ref[0], place_ref[1]
    panel = along * 2 + core
    for side in range(2):
        for way in range(ways):
            piece = pieces[side * ways + way]
            at = ((core ^ side) * ways + (along ^ way)) * piece.shape[0]
            for group in range(piece.shape[0]):
                lanes = pl.ds(pl.multiple_of((at + group) * LANES, LANES), LANES)
                picked = pick_rows(piece[group], panel, share_ref.shape[0])
                share_ref[:, lanes] = picked.astype(share_ref.dtype)


def cut_last_kernel(ways, place_ref, *refs):
    cut_rows(place_ref, refs[:-1], refs[-1])


def add_products(entry_ref, scale_ref, load, block_refs, total, adjoint, copies=()):
    total[...] = jnp.zeros_like(total)
    at = 0
    for block_ref in block_refs:
        for slot in range(block_ref.shape[0]):
            for start, copy in copies:
                if start == at:
                    copy.wait()
            row, col, scale = entry_ref[2 * at], entry_ref[2 * at + 1], scale_ref[at]
            at += 1
            source, target = (row, col) if adjoint else (col, row)
            term = lax.dot_general(
                load(source),
                block_ref[slot],
                (((1,), (0 if adjoint else 1,)), ((), ())),
                preferred_element_type=jnp.float32,
            )
            term = term * scale
            for piece in range(PER):
                total[target * PER + piece] += term[:, piece * LANES : (piece + 1) * LANES]


def load_from(x):
    def load(block):
        return jnp.concatenate([x[block * PER + piece] for piece in range(PER)], axis=1)

    return load


def write_parts(total, outs):
    at = 0
    for out_ref in outs:
        size = out_ref.shape[0]
        out_ref[...] = total[at : at + size].astype(out_ref.dtype)
        at += size


def join_parts(x, parts):
    at = 0
    for part in parts:
        size = part.shape[0]
        x[at : at + size] = part[...]
        at += size


def first_kernel(ways, entry_ref, scale_ref, place_ref, *refs):
    count = 2 * ways
    pieces, ready_ref, blocks_ref, outs = refs[:count], refs[count], refs[count + 1], refs[count + 2 : -5]
    total, wide, x, held_ref, sems = refs[-5:]
    copies = start_hold(blocks_ref, held_ref, sems)
    core, along = place_ref[0], place_ref[1]
    share, width = pieces[0].shape
    chunk = math.gcd(width, CHUNK)

    def assemble(step, carry):
        lanes = pl.ds(pl.multiple_of(step * chunk, chunk), chunk)
        rows = [piece[:, lanes].astype(jnp.float32) for piece in pieces]
        bit, place = 1, along + core * ways
        while bit < count:
            flip = (place & bit) != 0
            rows = [jnp.where(flip, rows[i ^ bit], rows[i]) for i in range(count)]
            bit *= 2
        for side in range(2):
            for way in range(ways):
                at = (2 * way + side) * share
                wide[at : at + share, lanes] = rows[side * ways + way]
        x[:, lanes] = wide[:, lanes].astype(x.dtype)
        return carry

    lax.fori_loop(0, width // chunk, assemble, 0)

    def load(block):
        return x[:, pl.ds(pl.multiple_of(block * B, B), B)]

    add_products(entry_ref, scale_ref, load, [ready_ref, held_ref], total, False, copies)
    write_parts(total, outs)


def forward_kernel(ways, entry_ref, scale_ref, place_ref, *refs):
    count = 2 * ways
    pieces, block_refs, outs = refs[:count], refs[count : count + 1], refs[count + 1 : -2]
    total, x = refs[-2:]
    core, along = place_ref[0], place_ref[1]
    size = pieces[0].shape[0]
    for side in range(2):
        for way in range(ways):
            at = ((core ^ side) * ways + (along ^ way)) * size
            x[pl.ds(at, size)] = pieces[side * ways + way][...]
    add_products(entry_ref, scale_ref, load_from(x), block_refs, total, False)
    write_parts(total, outs)


def adjoint_kernel(ways, entry_ref, scale_ref, place_ref, *refs):
    parts, block_refs = refs[:ROW_PARTS], refs[ROW_PARTS : ROW_PARTS + 1]
    outs = refs[ROW_PARTS + 1 : -2]
    total, x = refs[-2:]
    join_parts(x, parts)
    add_products(entry_ref, scale_ref, load_from(x), block_refs, total, True)
    core, along = place_ref[0], place_ref[1]
    size = outs[0].shape[1]
    for side, out_ref in enumerate(outs):
        for way in range(ways):
            at = ((core ^ side) * ways + (along ^ way)) * size
            out_ref[way] = total[pl.ds(at, size)].astype(out_ref.dtype)


def last_kernel(ways, entry_ref, scale_ref, place_ref, *refs):
    parts, block_refs = refs[:ROW_PARTS], refs[ROW_PARTS : ROW_PARTS + 1]
    out_ref, total, x = refs[ROW_PARTS + 1 :]
    join_parts(x, parts)
    add_products(entry_ref, scale_ref, load_from(x), block_refs, total, True)
    core, along = place_ref[0], place_ref[1]
    share = out_ref.shape[2]
    groups = math.gcd(total.shape[0], UNROLL)

    def write(step, carry):
        for i in range(groups):
            group = step * groups + i
            lanes = pl.ds(pl.multiple_of(group * LANES, LANES), LANES)
            values = total[group].astype(out_ref.dtype)
            for index in range(2 * ways):
                piece = values[index * share : (index + 1) * share]
                out_ref[core ^ (index % 2), along ^ (index // 2), :, lanes] = piece
        return carry

    lax.fori_loop(0, total.shape[0] // groups, write, 0)


def shards(strengths, blocks, pattern, level_gain):
    n_panel = lax.axis_size("panel")
    n_case = lax.axis_size("case")
    ways = n_panel // 2
    share, width = strengths.shape
    cases = share * n_panel
    slots = blocks.shape[0]
    col_blocks = width // B
    row_blocks = col_blocks * n_case // n_panel
    col_groups = col_blocks * PER
    row_groups = row_blocks * PER
    panel = lax.axis_index("panel")
    case = lax.axis_index("case")
    core = panel % 2
    along = panel // 2
    value = strengths.dtype
    row_cuts = spans(row_groups, ROW_PARTS)
    part_size = col_groups // n_panel

    place = jnp.stack([core, along, case]).astype(jnp.int32)
    first = jnp.stack([panel * row_blocks, case * col_blocks]).astype(jnp.int32)
    entry = jnp.where(pattern[:, 2:] >= 0, pattern[:, :2] - first, 0).reshape(-1)
    level_ids = jnp.arange(level_gain.shape[0], dtype=jnp.int32)
    scale = jnp.sum(jnp.where(pattern[:, 2:] == level_ids, level_gain, jnp.float32(0.0)), axis=1)

    smem = pl.BlockSpec(memory_space=pltpu.SMEM)
    vmem = pl.BlockSpec(memory_space=pltpu.VMEM)

    params = pltpu.CompilerParams(vmem_limit_bytes=VMEM_LIMIT)
    def cut(kernel, vectors, outs):
        return pl.pallas_call(
            functools.partial(kernel, ways),
            out_shape=[jax.ShapeDtypeStruct(shape, value) for shape in outs],
            in_specs=[smem] + [vmem] * len(vectors),
            out_specs=[vmem] * len(outs),
            compiler_params=params,
            cost_estimate=pl.CostEstimate(flops=0, bytes_accessed=8 * share * width, transcendentals=0),
        )(place, *vectors)

    def product(kernel, vectors, outs, scratch, limit=VMEM_LIMIT, space=None):
        small = (entry, scale, place)
        return pl.pallas_call(
            functools.partial(kernel, ways),
            out_shape=[jax.ShapeDtypeStruct(shape, value) for shape in outs],
            in_specs=[smem] * len(small) + [vmem] * len(vectors) + [space or vmem],
            out_specs=[vmem] * len(outs),
            scratch_shapes=scratch,
            compiler_params=pltpu.CompilerParams(vmem_limit_bytes=limit),
            cost_estimate=pl.CostEstimate(
                flops=2 * cases * slots * B * B, bytes_accessed=2 * slots * B * B, transcendentals=0
            ),
        )(*small, *vectors, blocks)

    def scratch(groups, kind):
        return pltpu.VMEM((groups, cases, LANES), kind)

    rows_total, rows_held = scratch(row_groups, jnp.float32), scratch(row_groups, value)
    cols_total, cols_held = scratch(col_groups, jnp.float32), scratch(col_groups, value)
    flat = [pltpu.VMEM((cases, width), kind) for kind in (jnp.float32, value)]
    row_shapes = [(size, cases, LANES) for _, size in row_cuts]

    def over_case(parts):
        bits = [1 << b for b in range(n_case.bit_length() - 1)]
        for step in range(len(bits)):
            by_core = [bits[(step + side) % len(bits)] for side in range(2)]
            pairs = [
                (p * n_case + c, p * n_case + (c ^ by_core[p % 2])) for p in range(n_panel) for c in range(n_case)
            ]
            parts = [add_up(part, lax.ppermute(part, ("panel", "case"), pairs)) for part in parts]
        return parts

    def scatter_panel(mine, theirs):
        return scatter_along(add_up(mine, swap(theirs, "panel", 1)))

    far_first = sorted(range(1, ways), key=lambda way: way & (ways // 2) == 0)

    def along_swaps(part_of):
        arrived = {way: swap(part_of(way), "panel", 2 * way) for way in far_first}
        return [arrived[way] for way in range(1, ways)]

    def scatter_along(summed):
        return add_up(summed[0], *along_swaps(lambda way: summed[way]))

    def gather_panel(part):
        same = [part, *along_swaps(lambda way: part)]
        return same + [swap(one, "panel", 1) for one in same]

    mine = jnp.where(core >= 0, strengths, 0)
    ready = jnp.where(core >= 0, blocks[: slots // 2], 0)
    own_copy = [pltpu.VMEM((slots - slots // 2, B, B), blocks.dtype), pltpu.SemaphoreType.DMA((COPIES,))]
    scratches = [rows_total, *flat, *own_copy]
    first_sums = over_case(
        product(first_kernel, [mine, *gather_panel(strengths)[1:], ready], row_shapes, scratches, FIRST_LIMIT, pl.BlockSpec(memory_space=pl.ANY))
    )
    outs = [(ways, part_size, cases, LANES)] * 2
    pieces = gather_panel(scatter_panel(*product(adjoint_kernel, first_sums, outs, [cols_total, rows_held])))
    sums = product(forward_kernel, pieces, row_shapes, [rows_total, cols_held])
    rows_out, share_out = (cases // n_case, row_groups * LANES), (share, width)
    sums, first_sums, pieces = lax.optimization_barrier((sums, first_sums, pieces))
    forward_one, adjoint_one = cut(cut_kernel, [*first_sums, *pieces], [rows_out, share_out])
    second_sums = over_case(sums)
    (by_share,) = product(last_kernel, second_sums, [(2, ways, share, width)], [cols_total, rows_held])
    summed = add_up(by_share[0], swap(by_share[1], "panel", 1))
    summed, second_sums = lax.optimization_barrier((summed, second_sums))
    adjoint_two = scatter_along(summed)
    (forward_two,) = cut(cut_last_kernel, second_sums, [rows_out])
    return (forward_one, adjoint_one, forward_two, adjoint_two)


def solution(mesh):
    in_specs = (
        P("panel", "case"),
        P(("panel", "case"), None, None),
        P(("panel", "case"), None),
        P(),
    )
    out_specs = (P("case", "panel"), P("panel", "case"), P("case", "panel"), P("panel", "case"))
    return jax.shard_map(shards, mesh=mesh, in_specs=in_specs, out_specs=out_specs, check_vma=False)
```

```python
import functools
import math

import jax
import jax.numpy as jnp
from jax import lax
from jax.experimental import pallas as pl
from jax.experimental.pallas import tpu as pltpu
from jax.sharding import PartitionSpec as P

B = 256
LANES = 128
PER = B // LANES
COPIES = 4
ROW_PARTS = 2
CHUNK = 1024
UNROLL = 96
VMEM_LIMIT = 12 * 1024 * 1024
FIRST_LIMIT = 50 * 1024 * 1024


def swap(value, axis, offset):
    count = lax.axis_size(axis)
    return lax.ppermute(value, axis, [(i, i ^ offset) for i in range(count)])


def add_up(*parts):
    total = parts[0].astype(jnp.float32)
    for part in parts[1:]:
        total = total + part.astype(jnp.float32)
    return total.astype(parts[0].dtype)


def spans(size, count):
    edges = [size * i // count for i in range(count + 1)]
    return [(a, b - a) for a, b in zip(edges, edges[1:])]


def start_hold(blocks_ref, held_ref, sems):
    size = held_ref.shape[0]
    before = blocks_ref.shape[0] - size
    copies = []
    for i, (start, count) in enumerate(spans(size, COPIES)):
        source = blocks_ref.at[pl.ds(before + start, count)]
        copy = pltpu.make_async_copy(source, held_ref.at[pl.ds(start, count)], sems.at[i])
        copy.start()
        copies.append((before + start, copy))
    return copies


def pick_rows(values, index, size):
    values = values.astype(jnp.float32)
    picked = values[:size]
    for i in range(1, values.shape[0] // size):
        picked = jnp.where(index == i, values[i * size : (i + 1) * size], picked)
    return picked


def cut_rows(place_ref, parts, out_ref):
    at = 0
    for part in parts:
        for group in range(part.shape[0]):
            picked = pick_rows(part[group], place_ref[2], out_ref.shape[0])
            out_ref[:, at : at + LANES] = picked.astype(out_ref.dtype)
            at += LANES


def cut_kernel(ways, place_ref, *refs):
    parts, pieces, (rows_ref, share_ref) = refs[:ROW_PARTS], refs[ROW_PARTS:-2], refs[-2:]
    cut_rows(place_ref, parts, rows_ref)
    core, along = place_ref[0], place_ref[1]
    panel = along * 2 + core
    for side in range(2):
        for way in range(ways):
            piece = pieces[side * ways + way]
            at = ((core ^ side) * ways + (along ^ way)) * piece.shape[0]
            for group in range(piece.shape[0]):
                lanes = pl.ds(pl.multiple_of((at + group) * LANES, LANES), LANES)
                picked = pick_rows(piece[group], panel, share_ref.shape[0])
                share_ref[:, lanes] = picked.astype(share_ref.dtype)


def cut_last_kernel(ways, place_ref, *refs):
    cut_rows(place_ref, refs[:-1], refs[-1])


def add_products(entry_ref, scale_ref, load, block_refs, total, adjoint, copies=()):
    total[...] = jnp.zeros_like(total)
    at = 0
    for block_ref in block_refs:
        for slot in range(block_ref.shape[0]):
            for start, copy in copies:
                if start == at:
                    copy.wait()
            row, col, scale = entry_ref[2 * at], entry_ref[2 * at + 1], scale_ref[at]
            at += 1
            source, target = (row, col) if adjoint else (col, row)
            term = lax.dot_general(
                load(source),
                block_ref[slot],
                (((1,), (0 if adjoint else 1,)), ((), ())),
                preferred_element_type=jnp.float32,
            )
            term = term * scale
            for piece in range(PER):
                total[target * PER + piece] += term[:, piece * LANES : (piece + 1) * LANES]


def load_from(x):
    def load(block):
        return jnp.concatenate([x[block * PER + piece] for piece in range(PER)], axis=1)

    return load


def write_parts(total, outs):
    at = 0
    for out_ref in outs:
        size = out_ref.shape[0]
        out_ref[...] = total[at : at + size].astype(out_ref.dtype)
        at += size


def join_parts(x, parts):
    at = 0
    for part in parts:
        size = part.shape[0]
        x[at : at + size] = part[...]
        at += size


def first_kernel(ways, entry_ref, scale_ref, place_ref, *refs):
    count = 2 * ways
    pieces, ready_ref, blocks_ref, outs = refs[:count], refs[count], refs[count + 1], refs[count + 2 : -5]
    total, wide, x, held_ref, sems = refs[-5:]
    copies = start_hold(blocks_ref, held_ref, sems)
    core, along = place_ref[0], place_ref[1]
    share, width = pieces[0].shape
    chunk = math.gcd(width, CHUNK)

    def assemble(step, carry):
        lanes = pl.ds(pl.multiple_of(step * chunk, chunk), chunk)
        rows = [piece[:, lanes].astype(jnp.float32) for piece in pieces]
        bit, place = 1, along + core * ways
        while bit < count:
            flip = (place & bit) != 0
            rows = [jnp.where(flip, rows[i ^ bit], rows[i]) for i in range(count)]
            bit *= 2
        for side in range(2):
            for way in range(ways):
                at = (2 * way + side) * share
                wide[at : at + share, lanes] = rows[side * ways + way]
        x[:, lanes] = wide[:, lanes].astype(x.dtype)
        return carry

    lax.fori_loop(0, width // chunk, assemble, 0)

    def load(block):
        return x[:, pl.ds(pl.multiple_of(block * B, B), B)]

    add_products(entry_ref, scale_ref, load, [ready_ref, held_ref], total, False, copies)
    write_parts(total, outs)


def forward_kernel(ways, entry_ref, scale_ref, place_ref, *refs):
    count = 2 * ways
    pieces, block_refs, outs = refs[:count], refs[count : count + 1], refs[count + 1 : -2]
    total, x = refs[-2:]
    core, along = place_ref[0], place_ref[1]
    size = pieces[0].shape[0]
    for side in range(2):
        for way in range(ways):
            at = ((core ^ side) * ways + (along ^ way)) * size
            x[pl.ds(at, size)] = pieces[side * ways + way][...]
    add_products(entry_ref, scale_ref, load_from(x), block_refs, total, False)
    write_parts(total, outs)


def adjoint_kernel(ways, entry_ref, scale_ref, place_ref, *refs):
    parts, block_refs = refs[:ROW_PARTS], refs[ROW_PARTS : ROW_PARTS + 1]
    outs = refs[ROW_PARTS + 1 : -2]
    total, x = refs[-2:]
    join_parts(x, parts)
    add_products(entry_ref, scale_ref, load_from(x), block_refs, total, True)
    core, along = place_ref[0], place_ref[1]
    size = outs[0].shape[1]
    for side, out_ref in enumerate(outs):
        for way in range(ways):
            at = ((core ^ side) * ways + (along ^ way)) * size
            out_ref[way] = total[pl.ds(at, size)].astype(out_ref.dtype)


def last_kernel(ways, entry_ref, scale_ref, place_ref, *refs):
    parts, block_refs = refs[:ROW_PARTS], refs[ROW_PARTS : ROW_PARTS + 1]
    out_ref, total, x = refs[ROW_PARTS + 1 :]
    join_parts(x, parts)
    add_products(entry_ref, scale_ref, load_from(x), block_refs, total, True)
    core, along = place_ref[0], place_ref[1]
    share = out_ref.shape[2]
    groups = math.gcd(total.shape[0], UNROLL)

    def write(step, carry):
        for i in range(groups):
            group = step * groups + i
            lanes = pl.ds(pl.multiple_of(group * LANES, LANES), LANES)
            values = total[group].astype(out_ref.dtype)
            for index in range(2 * ways):
                piece = values[index * share : (index + 1) * share]
                out_ref[core ^ (index % 2), along ^ (index // 2), :, lanes] = piece
        return carry

    lax.fori_loop(0, total.shape[0] // groups, write, 0)


def shards(strengths, blocks, pattern, level_gain):
    n_panel = lax.axis_size("panel")
    n_case = lax.axis_size("case")
    ways = n_panel // 2
    share, width = strengths.shape
    cases = share * n_panel
    slots = blocks.shape[0]
    col_blocks = width // B
    row_blocks = col_blocks * n_case // n_panel
    col_groups = col_blocks * PER
    row_groups = row_blocks * PER
    panel = lax.axis_index("panel")
    case = lax.axis_index("case")
    core = panel % 2
    along = panel // 2
    value = strengths.dtype
    row_cuts = spans(row_groups, ROW_PARTS)
    part_size = col_groups // n_panel

    place = jnp.stack([core, along, case]).astype(jnp.int32)
    first = jnp.stack([panel * row_blocks, case * col_blocks]).astype(jnp.int32)
    entry = jnp.where(pattern[:, 2:] >= 0, pattern[:, :2] - first, 0).reshape(-1)
    level_ids = jnp.arange(level_gain.shape[0], dtype=jnp.int32)
    scale = jnp.sum(jnp.where(pattern[:, 2:] == level_ids, level_gain, jnp.float32(0.0)), axis=1)

    smem = pl.BlockSpec(memory_space=pltpu.SMEM)
    vmem = pl.BlockSpec(memory_space=pltpu.VMEM)

    params = pltpu.CompilerParams(vmem_limit_bytes=VMEM_LIMIT)
    def cut(kernel, vectors, outs):
        return pl.pallas_call(
            functools.partial(kernel, ways),
            out_shape=[jax.ShapeDtypeStruct(shape, value) for shape in outs],
            in_specs=[smem] + [vmem] * len(vectors),
            out_specs=[vmem] * len(outs),
            compiler_params=params,
            cost_estimate=pl.CostEstimate(flops=0, bytes_accessed=8 * share * width, transcendentals=0),
        )(place, *vectors)

    def product(kernel, vectors, outs, scratch, limit=VMEM_LIMIT, space=None):
        small = (entry, scale, place)
        return pl.pallas_call(
            functools.partial(kernel, ways),
            out_shape=[jax.ShapeDtypeStruct(shape, value) for shape in outs],
            in_specs=[smem] * len(small) + [vmem] * len(vectors) + [space or vmem],
            out_specs=[vmem] * len(outs),
            scratch_shapes=scratch,
            compiler_params=pltpu.CompilerParams(vmem_limit_bytes=limit),
            cost_estimate=pl.CostEstimate(
                flops=2 * cases * slots * B * B, bytes_accessed=2 * slots * B * B, transcendentals=0
            ),
        )(*small, *vectors, blocks)

    def scratch(groups, kind):
        return pltpu.VMEM((groups, cases, LANES), kind)

    rows_total, rows_held = scratch(row_groups, jnp.float32), scratch(row_groups, value)
    cols_total, cols_held = scratch(col_groups, jnp.float32), scratch(col_groups, value)
    flat = [pltpu.VMEM((cases, width), kind) for kind in (jnp.float32, value)]
    row_shapes = [(size, cases, LANES) for _, size in row_cuts]

    def over_case(parts):
        bits = [1 << b for b in range(n_case.bit_length() - 1)]
        parts = list(parts)
        for step in range(len(bits)):
            arrived = [swap(part, "case", bits[(step + i) % len(bits)]) for i, part in enumerate(parts)]
            parts = [add_up(part, one) for part, one in zip(parts, arrived)]
        return parts

    def scatter_panel(mine, theirs):
        return scatter_along(add_up(mine, swap(theirs, "panel", 1)))

    far_first = sorted(range(1, ways), key=lambda way: way & (ways // 2) == 0)

    def along_swaps(part_of):
        arrived = {way: swap(part_of(way), "panel", 2 * way) for way in far_first}
        return [arrived[way] for way in range(1, ways)]

    def scatter_along(summed):
        return add_up(summed[0], *along_swaps(lambda way: summed[way]))

    def gather_panel(part):
        same = [part, *along_swaps(lambda way: part)]
        return same + [swap(one, "panel", 1) for one in same]

    mine = jnp.where(core >= 0, strengths, 0)
    at_hand = slots * 3 // 4
    ready = jnp.where(core >= 0, blocks[:at_hand], 0)
    own_copy = [pltpu.VMEM((slots - at_hand, B, B), blocks.dtype), pltpu.SemaphoreType.DMA((COPIES,))]
    scratches = [rows_total, *flat, *own_copy]
    first_sums = over_case(
        product(first_kernel, [mine, *gather_panel(strengths)[1:], ready], row_shapes, scratches, FIRST_LIMIT, pl.BlockSpec(memory_space=pl.ANY))
    )
    outs = [(ways, part_size, cases, LANES)] * 2
    pieces = gather_panel(scatter_panel(*product(adjoint_kernel, first_sums, outs, [cols_total, rows_held])))
    sums = product(forward_kernel, pieces, row_shapes, [rows_total, cols_held])
    rows_out, share_out = (cases // n_case, row_groups * LANES), (share, width)
    sums, first_sums, pieces = lax.optimization_barrier((sums, first_sums, pieces))
    forward_one, adjoint_one = cut(cut_kernel, [*first_sums, *pieces], [rows_out, share_out])
    second_sums = over_case(sums)
    (by_share,) = product(last_kernel, second_sums, [(2, ways, share, width)], [cols_total, rows_held])
    summed = add_up(by_share[0], swap(by_share[1], "panel", 1))
    summed, second_sums = lax.optimization_barrier((summed, second_sums))
    adjoint_two = scatter_along(summed)
    (forward_two,) = cut(cut_last_kernel, second_sums, [rows_out])
    return (forward_one, adjoint_one, forward_two, adjoint_two)


def solution(mesh):
    in_specs = (
        P("panel", "case"),
        P(("panel", "case"), None, None),
        P(("panel", "case"), None),
        P(),
    )
    out_specs = (P("case", "panel"), P("panel", "case"), P("case", "panel"), P("panel", "case"))
    return jax.shard_map(shards, mesh=mesh, in_specs=in_specs, out_specs=out_specs, check_vma=False)
```

```python
import functools
import math

import jax
import jax.numpy as jnp
from jax import lax
from jax.experimental import pallas as pl
from jax.experimental.pallas import tpu as pltpu
from jax.sharding import PartitionSpec as P

B = 256
LANES = 128
PER = B // LANES
COPIES = 4
ROW_PARTS = 2
CHUNK = 1024
UNROLL = 96
VMEM_LIMIT = 12 * 1024 * 1024
FIRST_LIMIT = 48 * 1024 * 1024


def swap(value, axis, offset):
    count = lax.axis_size(axis)
    return lax.ppermute(value, axis, [(i, i ^ offset) for i in range(count)])


def add_up(*parts):
    total = parts[0].astype(jnp.float32)
    for part in parts[1:]:
        total = total + part.astype(jnp.float32)
    return total.astype(parts[0].dtype)


def spans(size, count):
    edges = [size * i // count for i in range(count + 1)]
    return [(a, b - a) for a, b in zip(edges, edges[1:])]


def start_hold(blocks_ref, held_ref, sems):
    size = held_ref.shape[0]
    before = blocks_ref.shape[0] - size
    copies = []
    for i, (start, count) in enumerate(spans(size, COPIES)):
        source = blocks_ref.at[pl.ds(before + start, count)]
        copy = pltpu.make_async_copy(source, held_ref.at[pl.ds(start, count)], sems.at[i])
        copy.start()
        copies.append((before + start, copy))
    return copies


def pick_rows(values, index, size):
    values = values.astype(jnp.float32)
    picked = values[:size]
    for i in range(1, values.shape[0] // size):
        picked = jnp.where(index == i, values[i * size : (i + 1) * size], picked)
    return picked


def cut_rows(place_ref, parts, out_ref):
    at = 0
    for part in parts:
        for group in range(part.shape[0]):
            picked = pick_rows(part[group], place_ref[2], out_ref.shape[0])
            out_ref[:, at : at + LANES] = picked.astype(out_ref.dtype)
            at += LANES


def cut_kernel(ways, place_ref, *refs):
    parts, pieces, (rows_ref, share_ref) = refs[:ROW_PARTS], refs[ROW_PARTS:-2], refs[-2:]
    cut_rows(place_ref, parts, rows_ref)
    core, along = place_ref[0], place_ref[1]
    panel = along * 2 + core
    for side in range(2):
        for way in range(ways):
            piece = pieces[side * ways + way]
            at = ((core ^ side) * ways + (along ^ way)) * piece.shape[0]
            for group in range(piece.shape[0]):
                lanes = pl.ds(pl.multiple_of((at + group) * LANES, LANES), LANES)
                picked = pick_rows(piece[group], panel, share_ref.shape[0])
                share_ref[:, lanes] = picked.astype(share_ref.dtype)


def cut_last_kernel(ways, place_ref, *refs):
    cut_rows(place_ref, refs[:-1], refs[-1])


def add_products(entry_ref, scale_ref, load, block_refs, total, adjoint, copies=()):
    total[...] = jnp.zeros_like(total)
    at = 0
    for block_ref in block_refs:
        for slot in range(block_ref.shape[0]):
            for start, copy in copies:
                if start == at:
                    copy.wait()
            row, col, scale = entry_ref[2 * at], entry_ref[2 * at + 1], scale_ref[at]
            at += 1
            source, target = (row, col) if adjoint else (col, row)
            term = lax.dot_general(
                load(source),
                block_ref[slot],
                (((1,), (0 if adjoint else 1,)), ((), ())),
                preferred_element_type=jnp.float32,
            )
            term = term * scale
            for piece in range(PER):
                total[target * PER + piece] += term[:, piece * LANES : (piece + 1) * LANES]


def load_from(x):
    def load(block):
        return jnp.concatenate([x[block * PER + piece] for piece in range(PER)], axis=1)

    return load


def write_parts(total, outs):
    at = 0
    for out_ref in outs:
        size = out_ref.shape[0]
        out_ref[...] = total[at : at + size].astype(out_ref.dtype)
        at += size


def join_parts(x, parts):
    at = 0
    for part in parts:
        size = part.shape[0]
        x[at : at + size] = part[...]
        at += size


def first_kernel(ways, entry_ref, scale_ref, place_ref, *refs):
    count = 2 * ways
    pieces, ready_ref, blocks_ref, outs = refs[:count], refs[count], refs[count + 1], refs[count + 2 : -5]
    total, wide, x, held_ref, sems = refs[-5:]
    copies = start_hold(blocks_ref, held_ref, sems)
    core, along = place_ref[0], place_ref[1]
    share, width = pieces[0].shape
    chunk = math.gcd(width, CHUNK)

    def assemble(step, carry):
        lanes = pl.ds(pl.multiple_of(step * chunk, chunk), chunk)
        rows = [piece[:, lanes].astype(jnp.float32) for piece in pieces]
        bit, place = 1, along + core * ways
        while bit < count:
            flip = (place & bit) != 0
            rows = [jnp.where(flip, rows[i ^ bit], rows[i]) for i in range(count)]
            bit *= 2
        for side in range(2):
            for way in range(ways):
                at = (2 * way + side) * share
                wide[at : at + share, lanes] = rows[side * ways + way]
        x[:, lanes] = wide[:, lanes].astype(x.dtype)
        return carry

    lax.fori_loop(0, width // chunk, assemble, 0)

    def load(block):
        return x[:, pl.ds(pl.multiple_of(block * B, B), B)]

    add_products(entry_ref, scale_ref, load, [ready_ref, held_ref], total, False, copies)
    write_parts(total, outs)


def forward_kernel(ways, entry_ref, scale_ref, place_ref, *refs):
    count = 2 * ways
    pieces, block_refs, outs = refs[:count], refs[count : count + 1], refs[count + 1 : -2]
    total, x = refs[-2:]
    core, along = place_ref[0], place_ref[1]
    size = pieces[0].shape[0]
    for side in range(2):
        for way in range(ways):
            at = ((core ^ side) * ways + (along ^ way)) * size
            x[pl.ds(at, size)] = pieces[side * ways + way][...]
    add_products(entry_ref, scale_ref, load_from(x), block_refs, total, False)
    write_parts(total, outs)


def adjoint_kernel(ways, entry_ref, scale_ref, place_ref, *refs):
    parts, block_refs = refs[:ROW_PARTS], refs[ROW_PARTS : ROW_PARTS + 1]
    outs = refs[ROW_PARTS + 1 : -2]
    total, x = refs[-2:]
    join_parts(x, parts)
    add_products(entry_ref, scale_ref, load_from(x), block_refs, total, True)
    core, along = place_ref[0], place_ref[1]
    size = outs[0].shape[1]
    for side, out_ref in enumerate(outs):
        for way in range(ways):
            at = ((core ^ side) * ways + (along ^ way)) * size
            out_ref[way] = total[pl.ds(at, size)].astype(out_ref.dtype)


def last_kernel(ways, entry_ref, scale_ref, place_ref, *refs):
    parts, block_refs = refs[:ROW_PARTS], refs[ROW_PARTS : ROW_PARTS + 1]
    out_ref, total, x = refs[ROW_PARTS + 1 :]
    join_parts(x, parts)
    add_products(entry_ref, scale_ref, load_from(x), block_refs, total, True)
    core, along = place_ref[0], place_ref[1]
    share = out_ref.shape[2]
    groups = math.gcd(total.shape[0], UNROLL)

    def write(step, carry):
        for i in range(groups):
            group = step * groups + i
            lanes = pl.ds(pl.multiple_of(group * LANES, LANES), LANES)
            values = total[group].astype(out_ref.dtype)
            for index in range(2 * ways):
                piece = values[index * share : (index + 1) * share]
                out_ref[core ^ (index % 2), along ^ (index // 2), :, lanes] = piece
        return carry

    lax.fori_loop(0, total.shape[0] // groups, write, 0)


def shards(strengths, blocks, pattern, level_gain):
    n_panel = lax.axis_size("panel")
    n_case = lax.axis_size("case")
    ways = n_panel // 2
    share, width = strengths.shape
    cases = share * n_panel
    slots = blocks.shape[0]
    col_blocks = width // B
    row_blocks = col_blocks * n_case // n_panel
    col_groups = col_blocks * PER
    row_groups = row_blocks * PER
    panel = lax.axis_index("panel")
    case = lax.axis_index("case")
    core = panel % 2
    along = panel // 2
    value = strengths.dtype
    row_cuts = spans(row_groups, ROW_PARTS)
    part_size = col_groups // n_panel

    place = jnp.stack([core, along, case]).astype(jnp.int32)
    first = jnp.stack([panel * row_blocks, case * col_blocks]).astype(jnp.int32)
    entry = jnp.where(pattern[:, 2:] >= 0, pattern[:, :2] - first, 0).reshape(-1)
    level_ids = jnp.arange(level_gain.shape[0], dtype=jnp.int32)
    scale = jnp.sum(jnp.where(pattern[:, 2:] == level_ids, level_gain, jnp.float32(0.0)), axis=1)

    smem = pl.BlockSpec(memory_space=pltpu.SMEM)
    vmem = pl.BlockSpec(memory_space=pltpu.VMEM)

    params = pltpu.CompilerParams(vmem_limit_bytes=VMEM_LIMIT)
    def cut(kernel, vectors, outs):
        return pl.pallas_call(
            functools.partial(kernel, ways),
            out_shape=[jax.ShapeDtypeStruct(shape, value) for shape in outs],
            in_specs=[smem] + [vmem] * len(vectors),
            out_specs=[vmem] * len(outs),
            compiler_params=params,
            cost_estimate=pl.CostEstimate(flops=0, bytes_accessed=8 * share * width, transcendentals=0),
        )(place, *vectors)

    def product(kernel, vectors, outs, scratch, limit=VMEM_LIMIT, space=None):
        small = (entry, scale, place)
        return pl.pallas_call(
            functools.partial(kernel, ways),
            out_shape=[jax.ShapeDtypeStruct(shape, value) for shape in outs],
            in_specs=[smem] * len(small) + [vmem] * len(vectors) + [space or vmem],
            out_specs=[vmem] * len(outs),
            scratch_shapes=scratch,
            compiler_params=pltpu.CompilerParams(vmem_limit_bytes=limit),
            cost_estimate=pl.CostEstimate(
                flops=2 * cases * slots * B * B, bytes_accessed=2 * slots * B * B, transcendentals=0
            ),
        )(*small, *vectors, blocks)

    def scratch(groups, kind):
        return pltpu.VMEM((groups, cases, LANES), kind)

    rows_total, rows_held = scratch(row_groups, jnp.float32), scratch(row_groups, value)
    cols_total, cols_held = scratch(col_groups, jnp.float32), scratch(col_groups, value)
    flat = [pltpu.VMEM((cases, width), kind) for kind in (jnp.float32, value)]
    row_shapes = [(size, cases, LANES) for _, size in row_cuts]

    def over_case(parts):
        bits = [1 << b for b in range(n_case.bit_length() - 1)]
        parts = list(parts)
        for step in range(len(bits)):
            arrived = [swap(part, "case", bits[(step + i) % len(bits)]) for i, part in enumerate(parts)]
            parts = [add_up(part, one) for part, one in zip(parts, arrived)]
        return parts

    def scatter_panel(mine, theirs):
        return scatter_along(add_up(mine, swap(theirs, "panel", 1)))

    far_first = sorted(range(1, ways), key=lambda way: way & (ways // 2) == 0)

    def along_swaps(part_of):
        arrived = {way: swap(part_of(way), "panel", 2 * way) for way in far_first}
        return [arrived[way] for way in range(1, ways)]

    def scatter_along(summed):
        return add_up(summed[0], *along_swaps(lambda way: summed[way]))

    def gather_panel(part):
        same = [part, *along_swaps(lambda way: part)]
        return same + [swap(one, "panel", 1) for one in same]

    mine = jnp.where(core >= 0, strengths, 0)
    at_hand = slots * 3 // 4
    ready = jnp.where(core >= 0, blocks[:at_hand], 0)
    own_copy = [pltpu.VMEM((slots - at_hand, B, B), blocks.dtype), pltpu.SemaphoreType.DMA((COPIES,))]
    scratches = [rows_total, *flat, *own_copy]
    first_sums = over_case(
        product(first_kernel, [mine, *gather_panel(strengths)[1:], ready], row_shapes, scratches, FIRST_LIMIT, pl.BlockSpec(memory_space=pl.ANY))
    )
    outs = [(ways, part_size, cases, LANES)] * 2
    pieces = gather_panel(scatter_panel(*product(adjoint_kernel, first_sums, outs, [cols_total, rows_held])))
    sums = product(forward_kernel, pieces, row_shapes, [rows_total, cols_held])
    rows_out, share_out = (cases // n_case, row_groups * LANES), (share, width)
    sums, first_sums, pieces = lax.optimization_barrier((sums, first_sums, pieces))
    forward_one, adjoint_one = cut(cut_kernel, [*first_sums, *pieces], [rows_out, share_out])
    second_sums = over_case(sums)
    (by_share,) = product(last_kernel, second_sums, [(2, ways, share, width)], [cols_total, rows_held])
    summed = add_up(by_share[0], swap(by_share[1], "panel", 1))
    summed, second_sums = lax.optimization_barrier((summed, second_sums))
    adjoint_two = scatter_along(summed)
    (forward_two,) = cut(cut_last_kernel, second_sums, [rows_out])
    return (forward_one, adjoint_one, forward_two, adjoint_two)


def solution(mesh):
    in_specs = (
        P("panel", "case"),
        P(("panel", "case"), None, None),
        P(("panel", "case"), None),
        P(),
    )
    out_specs = (P("case", "panel"), P("panel", "case"), P("case", "panel"), P("panel", "case"))
    return jax.shard_map(shards, mesh=mesh, in_specs=in_specs, out_specs=out_specs, check_vma=False)
```

```python
import functools
import math

import jax
import jax.numpy as jnp
from jax import lax
from jax.experimental import pallas as pl
from jax.experimental.pallas import tpu as pltpu
from jax.sharding import PartitionSpec as P

B = 256
LANES = 128
PER = B // LANES
COPIES = 4
ROW_PARTS = 2
CHUNK = 1024
UNROLL = 96
VMEM_LIMIT = 12 * 1024 * 1024
FIRST_LIMIT = 50 * 1024 * 1024


def swap(value, axis, offset):
    count = lax.axis_size(axis)
    return lax.ppermute(value, axis, [(i, i ^ offset) for i in range(count)])


def add_up(*parts):
    total = parts[0].astype(jnp.float32)
    for part in parts[1:]:
        total = total + part.astype(jnp.float32)
    return total.astype(parts[0].dtype)


def spans(size, count):
    edges = [size * i // count for i in range(count + 1)]
    return [(a, b - a) for a, b in zip(edges, edges[1:])]


def start_hold(blocks_ref, held_ref, sems):
    size = held_ref.shape[0]
    before = blocks_ref.shape[0] - size
    copies = []
    for i, (start, count) in enumerate(spans(size, COPIES)):
        source = blocks_ref.at[pl.ds(before + start, count)]
        copy = pltpu.make_async_copy(source, held_ref.at[pl.ds(start, count)], sems.at[i])
        copy.start()
        copies.append((before + start, copy))
    return copies


def pick_rows(values, index, size):
    values = values.astype(jnp.float32)
    picked = values[:size]
    for i in range(1, values.shape[0] // size):
        picked = jnp.where(index == i, values[i * size : (i + 1) * size], picked)
    return picked


def cut_rows(place_ref, parts, out_ref):
    at = 0
    for part in parts:
        for group in range(part.shape[0]):
            picked = pick_rows(part[group], place_ref[2], out_ref.shape[0])
            out_ref[:, at : at + LANES] = picked.astype(out_ref.dtype)
            at += LANES


def cut_kernel(ways, place_ref, *refs):
    parts, pieces, (rows_ref, share_ref) = refs[:ROW_PARTS], refs[ROW_PARTS:-2], refs[-2:]
    cut_rows(place_ref, parts, rows_ref)
    core, along = place_ref[0], place_ref[1]
    panel = along * 2 + core
    for side in range(2):
        for way in range(ways):
            piece = pieces[side * ways + way]
            at = ((core ^ side) * ways + (along ^ way)) * piece.shape[0]
            for group in range(piece.shape[0]):
                lanes = pl.ds(pl.multiple_of((at + group) * LANES, LANES), LANES)
                picked = pick_rows(piece[group], panel, share_ref.shape[0])
                share_ref[:, lanes] = picked.astype(share_ref.dtype)


def cut_last_kernel(ways, place_ref, *refs):
    cut_rows(place_ref, refs[:-1], refs[-1])


def add_products(entry_ref, scale_ref, load, block_refs, total, adjoint, copies=()):
    total[...] = jnp.zeros_like(total)
    at = 0
    for block_ref in block_refs:
        for slot in range(block_ref.shape[0]):
            for start, copy in copies:
                if start == at:
                    copy.wait()
            row, col, scale = entry_ref[2 * at], entry_ref[2 * at + 1], scale_ref[at]
            at += 1
            source, target = (row, col) if adjoint else (col, row)
            term = lax.dot_general(
                load(source),
                block_ref[slot],
                (((1,), (0 if adjoint else 1,)), ((), ())),
                preferred_element_type=jnp.float32,
            )
            term = term * scale
            for piece in range(PER):
                total[target * PER + piece] += term[:, piece * LANES : (piece + 1) * LANES]


def load_from(x):
    def load(block):
        return jnp.concatenate([x[block * PER + piece] for piece in range(PER)], axis=1)

    return load


def write_parts(total, outs):
    at = 0
    for out_ref in outs:
        size = out_ref.shape[0]
        out_ref[...] = total[at : at + size].astype(out_ref.dtype)
        at += size


def join_parts(x, parts):
    at = 0
    for part in parts:
        size = part.shape[0]
        x[at : at + size] = part[...]
        at += size


def first_kernel(ways, entry_ref, scale_ref, place_ref, *refs):
    count = 2 * ways
    pieces, ready_ref, blocks_ref, outs = refs[:count], refs[count], refs[count + 1], refs[count + 2 : -5]
    total, wide, x, held_ref, sems = refs[-5:]
    copies = start_hold(blocks_ref, held_ref, sems)
    core, along = place_ref[0], place_ref[1]
    share, width = pieces[0].shape
    chunk = math.gcd(width, CHUNK)

    def assemble(step, carry):
        lanes = pl.ds(pl.multiple_of(step * chunk, chunk), chunk)
        rows = [piece[:, lanes].astype(jnp.float32) for piece in pieces]
        bit, place = 1, along + core * ways
        while bit < count:
            flip = (place & bit) != 0
            rows = [jnp.where(flip, rows[i ^ bit], rows[i]) for i in range(count)]
            bit *= 2
        for side in range(2):
            for way in range(ways):
                at = (2 * way + side) * share
                wide[at : at + share, lanes] = rows[side * ways + way]
        x[:, lanes] = wide[:, lanes].astype(x.dtype)
        return carry

    lax.fori_loop(0, width // chunk, assemble, 0)

    def load(block):
        return x[:, pl.ds(pl.multiple_of(block * B, B), B)]

    add_products(entry_ref, scale_ref, load, [ready_ref, held_ref], total, False, copies)
    write_parts(total, outs)


def forward_kernel(ways, entry_ref, scale_ref, place_ref, *refs):
    count = 2 * ways
    pieces, block_refs, outs = refs[:count], refs[count : count + 1], refs[count + 1 : -2]
    total, x = refs[-2:]
    core, along = place_ref[0], place_ref[1]
    size = pieces[0].shape[0]
    for side in range(2):
        for way in range(ways):
            at = ((core ^ side) * ways + (along ^ way)) * size
            x[pl.ds(at, size)] = pieces[side * ways + way][...]
    add_products(entry_ref, scale_ref, load_from(x), block_refs, total, False)
    write_parts(total, outs)


def adjoint_kernel(ways, entry_ref, scale_ref, place_ref, *refs):
    parts, block_refs = refs[:ROW_PARTS], refs[ROW_PARTS : ROW_PARTS + 1]
    outs = refs[ROW_PARTS + 1 : -2]
    total, x = refs[-2:]
    join_parts(x, parts)
    add_products(entry_ref, scale_ref, load_from(x), block_refs, total, True)
    core, along = place_ref[0], place_ref[1]
    size = outs[0].shape[1]
    for side, out_ref in enumerate(outs):
        for way in range(ways):
            at = ((core ^ side) * ways + (along ^ way)) * size
            out_ref[way] = total[pl.ds(at, size)].astype(out_ref.dtype)


def last_kernel(ways, entry_ref, scale_ref, place_ref, *refs):
    parts, block_refs = refs[:ROW_PARTS], refs[ROW_PARTS : ROW_PARTS + 1]
    out_ref, total, x = refs[ROW_PARTS + 1 :]
    join_parts(x, parts)
    add_products(entry_ref, scale_ref, load_from(x), block_refs, total, True)
    core, along = place_ref[0], place_ref[1]
    share = out_ref.shape[2]
    groups = math.gcd(total.shape[0], UNROLL)

    def write(step, carry):
        for i in range(groups):
            group = step * groups + i
            lanes = pl.ds(pl.multiple_of(group * LANES, LANES), LANES)
            values = total[group].astype(out_ref.dtype)
            for index in range(2 * ways):
                piece = values[index * share : (index + 1) * share]
                out_ref[core ^ (index % 2), along ^ (index // 2), :, lanes] = piece
        return carry

    lax.fori_loop(0, total.shape[0] // groups, write, 0)


def shards(strengths, blocks, pattern, level_gain):
    n_panel = lax.axis_size("panel")
    n_case = lax.axis_size("case")
    ways = n_panel // 2
    share, width = strengths.shape
    cases = share * n_panel
    slots = blocks.shape[0]
    col_blocks = width // B
    row_blocks = col_blocks * n_case // n_panel
    col_groups = col_blocks * PER
    row_groups = row_blocks * PER
    panel = lax.axis_index("panel")
    case = lax.axis_index("case")
    core = panel % 2
    along = panel // 2
    value = strengths.dtype
    row_cuts = spans(row_groups, ROW_PARTS)
    part_size = col_groups // n_panel

    place = jnp.stack([core, along, case]).astype(jnp.int32)
    first = jnp.stack([panel * row_blocks, case * col_blocks]).astype(jnp.int32)
    entry = jnp.where(pattern[:, 2:] >= 0, pattern[:, :2] - first, 0).reshape(-1)
    level_ids = jnp.arange(level_gain.shape[0], dtype=jnp.int32)
    scale = jnp.sum(jnp.where(pattern[:, 2:] == level_ids, level_gain, jnp.float32(0.0)), axis=1)

    smem = pl.BlockSpec(memory_space=pltpu.SMEM)
    vmem = pl.BlockSpec(memory_space=pltpu.VMEM)

    params = pltpu.CompilerParams(vmem_limit_bytes=VMEM_LIMIT)
    def cut(kernel, vectors, outs):
        return pl.pallas_call(
            functools.partial(kernel, ways),
            out_shape=[jax.ShapeDtypeStruct(shape, value) for shape in outs],
            in_specs=[smem] + [vmem] * len(vectors),
            out_specs=[vmem] * len(outs),
            compiler_params=params,
            cost_estimate=pl.CostEstimate(flops=0, bytes_accessed=8 * share * width, transcendentals=0),
        )(place, *vectors)

    def product(kernel, vectors, outs, scratch, limit=VMEM_LIMIT, space=None):
        small = (entry, scale, place)
        return pl.pallas_call(
            functools.partial(kernel, ways),
            out_shape=[jax.ShapeDtypeStruct(shape, value) for shape in outs],
            in_specs=[smem] * len(small) + [vmem] * len(vectors) + [space or vmem],
            out_specs=[vmem] * len(outs),
            scratch_shapes=scratch,
            compiler_params=pltpu.CompilerParams(vmem_limit_bytes=limit),
            cost_estimate=pl.CostEstimate(
                flops=2 * cases * slots * B * B, bytes_accessed=2 * slots * B * B, transcendentals=0
            ),
        )(*small, *vectors, blocks)

    def scratch(groups, kind):
        return pltpu.VMEM((groups, cases, LANES), kind)

    rows_total, rows_held = scratch(row_groups, jnp.float32), scratch(row_groups, value)
    cols_total, cols_held = scratch(col_groups, jnp.float32), scratch(col_groups, value)
    flat = [pltpu.VMEM((cases, width), kind) for kind in (jnp.float32, value)]
    row_shapes = [(size, cases, LANES) for _, size in row_cuts]

    def over_case(parts):
        bits = [1 << b for b in range(n_case.bit_length() - 1)]
        parts = list(parts)
        for step in range(len(bits)):
            arrived = [swap(part, "case", bits[(step + i) % len(bits)]) for i, part in enumerate(parts)]
            parts = [add_up(part, one) for part, one in zip(parts, arrived)]
        return parts

    def scatter_panel(mine, theirs):
        return scatter_along(add_up(mine, swap(theirs, "panel", 1)))

    far_first = sorted(range(1, ways), key=lambda way: way & (ways // 2) == 0)

    def along_swaps(part_of):
        arrived = {way: swap(part_of(way), "panel", 2 * way) for way in far_first}
        return [arrived[way] for way in range(1, ways)]

    def scatter_along(summed):
        return add_up(summed[0], *along_swaps(lambda way: summed[way]))

    def gather_panel(part):
        same = [part, *along_swaps(lambda way: part)]
        return same + [swap(one, "panel", 1) for one in same]

    mine = jnp.where(core >= 0, strengths, 0)
    ready = jnp.where(core >= 0, blocks[: slots // 2], 0)
    own_copy = [pltpu.VMEM((slots - slots // 2, B, B), blocks.dtype), pltpu.SemaphoreType.DMA((COPIES,))]
    scratches = [rows_total, *flat, *own_copy]
    first_sums = over_case(
        product(first_kernel, [mine, *gather_panel(strengths)[1:], ready], row_shapes, scratches, FIRST_LIMIT, pl.BlockSpec(memory_space=pl.ANY))
    )
    outs = [(ways, part_size, cases, LANES)] * 2
    pieces = gather_panel(scatter_panel(*product(adjoint_kernel, first_sums, outs, [cols_total, rows_held])))
    sums = product(forward_kernel, pieces, row_shapes, [rows_total, cols_held])
    rows_out, share_out = (cases // n_case, row_groups * LANES), (share, width)
    sums, first_sums, pieces = lax.optimization_barrier((sums, first_sums, pieces))
    forward_one, adjoint_one = cut(cut_kernel, [*first_sums, *pieces], [rows_out, share_out])
    second_sums = over_case(sums)
    (by_share,) = product(last_kernel, second_sums, [(2, ways, share, width)], [cols_total, rows_held])
    summed = add_up(by_share[0], swap(by_share[1], "panel", 1))
    summed, second_sums = lax.optimization_barrier((summed, second_sums))
    adjoint_two = scatter_along(summed)
    (forward_two,) = cut(cut_last_kernel, second_sums, [rows_out])
    return (forward_one, adjoint_one, forward_two, adjoint_two)


def solution(mesh):
    in_specs = (
        P("panel", "case"),
        P(("panel", "case"), None, None),
        P(("panel", "case"), None),
        P(),
    )
    out_specs = (P("case", "panel"), P("panel", "case"), P("case", "panel"), P("panel", "case"))
    return jax.shard_map(shards, mesh=mesh, in_specs=in_specs, out_specs=out_specs, check_vma=False)
```
